32 devices in a mesh: blk: 16 (over z, x, core), col: 2 (over y).
Axes of the slice: x: 2, y: 2, z: 4, core: 2. Of those that a mesh axis runs over, the one named last changes fastest.
Arguments:
- tiles: bfloat16 [384, 128, 128], P('blk'), may hold values from -0.21875 to 0.21875
- tile_rows: int32 [384], P('blk'), may hold values from 0 to 3, as said below
- tile_cols: int32 [384], P('blk'), may hold values from 0 to 511, as said below
- tile_count: int32 [16], P('blk'), may hold values from 3 to 24, as said below
- sketch: bfloat16 [65536, 512], P('blk', 'col'), may hold values from -6 to 6
- variant_scale: bfloat16 [65536], P('blk'), may hold values from 0.5 to 2
Outputs:
- basis_rows: float32 [8192, 512], P('blk', 'col')
The draws below stay inside these ranges and needn't reach their ends.
Inputs may be any that keep to these rules, and one draw needn't show every extreme that they name: `tile_count`: each row group has 24, 12, 6 or 3 live slots, and at least one group has all 24 live. `tile_rows`: no two slots of a row group name the same block row and block column. Slots at or past their group's count are not part of the matrix. `tile_cols`: within one row group, all slots whose block columns lie in the same run of 32 block columns that starts at a multiple of 32 name the same block column.
All inputs are finite; a program needn't handle non-finite values.
Results may differ from the reference program's by a relative error of at most 0.0059.
Values may be sent and summed in bfloat16 or wider, within the bound.
A program may use at most 128 MiB of HBM per device.

```python
import math
import jax
import jax.numpy as jnp
from jax import lax

BLOCK = 128
K = 512
TPR = 6
RB_DEV = 4
VARIANTS = 65536
TILES = 24
GROUPS = 16
M = 8192


def pattern(key):
    own_blocks = VARIANTS // BLOCK // GROUPS
    exponents = jax.random.randint(jax.random.fold_in(key, 11), (GROUPS,), 0, 4)
    counts = TILES // jnp.left_shift(jnp.ones_like(exponents), exponents)
    chosen = jax.random.randint(jax.random.fold_in(key, 12), (), 0, GROUPS)
    counts = jnp.where(jnp.arange(GROUPS) == chosen, TILES, counts).astype(jnp.int32)
    group_keys = jax.random.split(jax.random.fold_in(key, 13), GROUPS)

    def one_group(group_key):
        picks = jax.random.randint(jax.random.fold_in(group_key, 1), (GROUPS,), 0, own_blocks)
        positions = jax.random.permutation(jax.random.fold_in(group_key, 2), RB_DEV * GROUPS)[:TILES]
        owners = positions % GROUPS
        return (positions // GROUPS, owners * own_blocks + jnp.take(picks, owners))
    row_index, col_index = jax.vmap(one_group)(group_keys)
    return (row_index.reshape(-1).astype(jnp.int32), col_index.reshape(-1).astype(jnp.int32), counts)


def draw_tile_rows(key, part):
    return pattern(key)[0]


def draw_tile_cols(key, part):
    return pattern(key)[1]


def draw_tile_count(key, part):
    return pattern(key)[2]


def block_scale(stream_key, dims, shards, least, high):
    def one(dim, shards_of):
        heights = jax.random.uniform(jax.random.fold_in(jax.random.fold_in(stream_key, 6), dim), (shards_of,), jnp.float32, least / len(shards), high / len(shards))
        return jnp.repeat(jnp.exp(heights), dims[dim] // shards_of).reshape((-1,) + (1,) * (len(dims) - dim - 1))

    gain = one(*shards[0])
    for cut in shards[1:]:
        gain = gain * one(*cut)
    return gain


def scatter_about(own_key, extent, scale, reach, cuts=(), kind=jnp.bfloat16):
    level = block_scale(own_key, extent, cuts, -0.22, 0.18) if cuts else 1.0
    entries = jax.random.normal(own_key, extent, jnp.float32) * scale * level
    return jnp.minimum(jnp.maximum(entries, -reach), reach).astype(kind)


def setup_inputs(seed: int = 0) -> dict:
    key_of = jax.random.split(jax.random.key(seed), 7)
    return {
        "tiles": scatter_about(key_of[0], (GROUPS * TILES, BLOCK, BLOCK), (TPR * BLOCK) ** -0.5, 0.21875, ((0, 16),)),
        "tile_rows": draw_tile_rows(jax.random.fold_in(key_of[6], 71), 0),
        "tile_cols": draw_tile_cols(jax.random.fold_in(key_of[6], 71), 0),
        "tile_count": draw_tile_count(jax.random.fold_in(key_of[6], 71), 0),
        "sketch": scatter_about(key_of[4], (VARIANTS, K), 1.0, 6.0, ((0, 16), (1, 2))),
        "variant_scale": jnp.clip(jnp.exp(math.log(2.0) - 1.3862944 * jax.random.uniform(key_of[5], (VARIANTS,), jnp.float32) ** block_scale(key_of[5], (VARIANTS,), ((0, 16),), -0.2, 0.2)), 0.5, 2.0).astype(jnp.bfloat16),
    }


def reference(tiles, tile_rows, tile_cols, tile_count, sketch, variant_scale):
    col_blocks = VARIANTS // BLOCK
    own_blocks = VARIANTS // BLOCK // GROUPS
    sketch_width = sketch.shape[1]
    tile_groups = tiles.reshape(GROUPS, TILES, BLOCK, BLOCK)
    row_groups = tile_rows.reshape(GROUPS, TILES)
    col_groups = tile_cols.reshape(GROUPS, TILES)
    slot_ids = jnp.arange(TILES, dtype=jnp.int32)
    live_masks = (slot_ids[None, :] < tile_count[:, None]).astype(jnp.float32)
    scales = variant_scale.astype(jnp.float32)
    scaled_sketch = (scales[:, None] * sketch.astype(jnp.float32)).astype(jnp.bfloat16)
    owner_ids = jnp.arange(GROUPS, dtype=jnp.int32)

    def forward(operand):
        blocks = operand.reshape(col_blocks, BLOCK, sketch_width)

        def one_group(pieces):
            tile_group, row_group, col_group, live_mask = pieces
            selected = jnp.take(blocks, col_group, axis=0).astype(jnp.float32)
            products = jnp.einsum('tij,tjk->tik', tile_group.astype(jnp.float32), selected) * live_mask[:, None, None]
            return jnp.zeros((RB_DEV, BLOCK, sketch_width), jnp.float32).at[row_group].add(products)
        result_rows = lax.map(one_group, (tile_groups, row_groups, col_groups, live_masks))
        return result_rows.reshape(GROUPS * RB_DEV * BLOCK, sketch_width)
    range_rows = forward(scaled_sketch).astype(jnp.bfloat16)

    def backward(accumulated, pieces):
        tile_group, row_group, col_group, live_mask, group_rows = pieces
        selected = jnp.take(group_rows, row_group, axis=0).astype(jnp.float32)
        products = jnp.einsum('tji,tjk->tik', tile_group.astype(jnp.float32), selected) * live_mask[:, None, None]
        slot_owner = (col_group // own_blocks).astype(jnp.int32)
        owner_term = jnp.zeros((GROUPS, BLOCK, sketch_width), jnp.float32).at[slot_owner].add(products)
        rounded = lax.optimization_barrier(owner_term.astype(jnp.bfloat16)).astype(jnp.float32)
        slot_hits = (slot_owner[None, :] == owner_ids[:, None]) & (live_mask[None, :] > 0.5)
        wanted = jnp.max(jnp.where(slot_hits, (col_group % own_blocks)[None, :], 0), axis=1).astype(jnp.int32)
        target = (owner_ids * own_blocks + wanted).astype(jnp.int32)
        return (accumulated.at[target].add(rounded), None)
    start_back = jnp.zeros((col_blocks, BLOCK, sketch_width), jnp.float32)
    back, _ = lax.scan(backward, start_back, (tile_groups, row_groups, col_groups, live_masks, range_rows.reshape(GROUPS, RB_DEV, BLOCK, sketch_width)))
    back = back.reshape(VARIANTS, sketch_width)
    weighted = ((scales * scales)[:, None] * back).astype(jnp.bfloat16)
    power_rows = forward(weighted).astype(jnp.bfloat16)
    gram = lax.dot_general(power_rows.astype(jnp.float32), power_rows.astype(jnp.float32), (((0,), (0,)), ((), ())), preferred_element_type=jnp.float32) / M
    lower_factor = jnp.linalg.cholesky(gram)
    identity = jnp.eye(sketch_width, dtype=jnp.float32)
    inverse = jax.scipy.linalg.solve_triangular(lower_factor, identity, lower=True)
    return jnp.dot(power_rows.astype(jnp.float32), inverse.T, precision=lax.Precision.HIGHEST)
```

```python
import functools
import jax
import jax.numpy as jnp
from jax import lax
from jax.experimental import pallas as pl
from jax.experimental.pallas import tpu as pltpu
from jax.sharding import PartitionSpec as P

TPR = 6
RB_DEV = 4
STEP = 3
PANEL = 8
VMEM_BYTES = 60 * 2**20
HIGHEST = lax.Precision.HIGHEST

SMEM_SPEC = pl.BlockSpec(memory_space=pltpu.SMEM)
VMEM_SPEC = pl.BlockSpec(memory_space=pltpu.VMEM)
PARAMS = pltpu.CompilerParams(vmem_limit_bytes=VMEM_BYTES)


def forward_rows(rows_ref, owner_ref, count, tiles_ref, fetched_ref, acc_ref):
    acc_ref[...] = jnp.zeros_like(acc_ref)

    def turn(index, carry):
        slots = [index * STEP + step for step in range(STEP)]
        products = [
            jnp.dot(
                tiles_ref[slot], fetched_ref[owner_ref[slot]], preferred_element_type=jnp.float32
            )
            for slot in slots
        ]
        for slot, product in zip(slots, products):
            acc_ref[rows_ref[slot]] += product
        return carry

    lax.fori_loop(0, count // STEP, turn, 0)


def range_kernel(rows_ref, owner_ref, count_ref, tiles_ref, fetched_ref, terms_ref, acc_ref, held_ref, sum_ref):
    count = count_ref[0]
    forward_rows(rows_ref, owner_ref, count, tiles_ref, fetched_ref, acc_ref)
    held_ref[...] = acc_ref[...].astype(jnp.bfloat16)
    sum_ref[...] = jnp.zeros_like(sum_ref)

    def turn(index, carry):
        slots = [index * STEP + step for step in range(STEP)]
        products = [
            lax.dot_general(
                tiles_ref[slot],
                held_ref[rows_ref[slot]],
                (((0,), (0,)), ((), ())),
                preferred_element_type=jnp.float32,
            )
            for slot in slots
        ]
        for slot, product in zip(slots, products):
            sum_ref[owner_ref[slot]] += product
        return carry

    lax.fori_loop(0, count // STEP, turn, 0)
    terms_ref[...] = sum_ref[...].astype(jnp.bfloat16)


def power_kernel(rows_ref, owner_ref, count_ref, tiles_ref, fetched_ref, out_ref, acc_ref):
    forward_rows(rows_ref, owner_ref, count_ref[0], tiles_ref, fetched_ref, acc_ref)
    out_ref[...] = acc_ref[...].astype(jnp.bfloat16)


def weight_kernel(asked_ref, square_ref, terms_ref, out_ref, sum_ref):
    owners, edge, width = terms_ref.shape

    def clear(q, carry):
        sum_ref[asked_ref[q]] = jnp.zeros((edge, width), jnp.float32)
        return carry

    def gather(q, carry):
        sum_ref[asked_ref[q]] += terms_ref[q].astype(jnp.float32)
        return carry

    def scale(q, carry):
        total = sum_ref[asked_ref[q]]
        for part in range(0, width, edge):
            out_ref[q, :, part : part + edge] = (
                square_ref[q] * total[:, part : part + edge]
            ).astype(jnp.bfloat16)
        return carry

    lax.fori_loop(0, owners, clear, 0)
    lax.fori_loop(0, owners, gather, 0)
    lax.fori_loop(0, owners, scale, 0)


def invert_block(block):
    edge = block.shape[0]
    lanes = lax.broadcasted_iota(jnp.int32, (PANEL, edge), 1)
    sublanes = lax.broadcasted_iota(jnp.int32, (PANEL, edge), 0)
    strips = [block[start : start + PANEL, :] for start in range(0, edge, PANEL)]
    done = []
    for panel in range(len(strips)):
        first = panel * PANEL
        live = strips[panel:]
        columns = [
            [
                jnp.broadcast_to(strip[:, first + k : first + k + 1], (PANEL, edge))
                for strip in live
            ]
            for k in range(PANEL)
        ]
        inside = (lanes >= first) & (lanes < first + PANEL)
        unit = (lanes == first + sublanes).astype(jnp.float32)
        live = [
            jnp.where(inside, unit if at == 0 else 0.0, strip) for at, strip in enumerate(live)
        ]
        pivots = jnp.ones((PANEL, edge), jnp.float32)
        for i in range(PANEL):
            pivot = jnp.broadcast_to(columns[i][0][i : i + 1, :], (PANEL, edge))
            pivots = jnp.where(sublanes == i, pivot, pivots)
            factor = 1.0 / pivot
            row = jnp.broadcast_to(live[0][i : i + 1, :], (PANEL, edge))
            heads = [
                jnp.broadcast_to(columns[k][0][i : i + 1, :], (PANEL, edge))
                for k in range(i + 1, PANEL)
            ]
            for at in range(len(live)):
                times = columns[i][at] * factor
                if at == 0:
                    times = jnp.where(sublanes > i, times, 0.0)
                live[at] = live[at] - times * row
                for k in range(i + 1, PANEL):
                    columns[k][at] = columns[k][at] - times * heads[k - i - 1]
        done.append(jnp.where(lanes <= first + sublanes, live[0] * lax.rsqrt(pivots), 0.0))
        strips = strips[: panel + 1] + live[1:]
    return jnp.concatenate(done, axis=0)


def basis_kernel(col_ref, gram_ref, rows_ref, out_ref, held_ref):
    size = gram_ref.shape[0]
    width = out_ref.shape[1]
    edge = 128
    held_ref[...] = gram_ref[...]
    for start in range(0, size, edge):
        stop = start + edge
        inverse = invert_block(held_ref[start:stop, start:stop])
        if start:
            before = jnp.dot(
                inverse, held_ref[start:stop, :start],
                precision=HIGHEST, preferred_element_type=jnp.float32,
            )
            held_ref[start:stop, :start] = before
        held_ref[start:stop, start:stop] = inverse
        if stop < size:
            panel = lax.dot_general(
                held_ref[stop:, start:stop], inverse, (((1,), (1,)), ((), ())),
                precision=HIGHEST, preferred_element_type=jnp.float32,
            )
            held_ref[stop:, stop:] -= lax.dot_general(
                panel, panel, (((1,), (1,)), ((), ())),
                precision=HIGHEST, preferred_element_type=jnp.float32,
            )
            if start:
                held_ref[stop:, :start] -= jnp.dot(
                    panel, before, precision=HIGHEST, preferred_element_type=jnp.float32
                )
            held_ref[stop:, start:stop] = -jnp.dot(
                panel, inverse, precision=HIGHEST, preferred_element_type=jnp.float32
            )
            held_ref[start:stop, stop:] = jnp.zeros((edge, size - stop), jnp.float32)
    first = pl.multiple_of(col_ref[0] * width, width)
    own = held_ref[pl.ds(first, width), :]
    high = own.astype(jnp.bfloat16)
    rest = own - high.astype(jnp.float32)
    middle = rest.astype(jnp.bfloat16)
    low = (rest - middle.astype(jnp.float32)).astype(jnp.bfloat16)
    total = jnp.zeros(out_ref.shape, jnp.float32)
    for piece in (low, middle, high):
        total += lax.dot_general(
            rows_ref[...], piece, (((1,), (1,)), ((), ())), preferred_element_type=jnp.float32
        )
    out_ref[...] = total


def from_partner(x, axis, apart):
    return lax.ppermute(x, axis, [(i, i ^ 1 << apart) for i in range(lax.axis_size(axis))])


def gram_of(row_block):
    return lax.dot_general(
        row_block, row_block, (((0,), (0,)), ((), ())), preferred_element_type=jnp.float32
    )


def local(tiles, tile_rows, tile_cols, tile_count, sketch, variant_scale):
    width = sketch.shape[1]
    edge = tiles.shape[1]
    owners = lax.axis_size("blk")
    own_blocks = sketch.shape[0] // edge
    own_rows = RB_DEV
    live_count = tile_count[0]
    every_slot = jnp.arange(tiles.shape[0], dtype=jnp.int32)
    owner_ids = jnp.arange(owners, dtype=jnp.int32)
    slot_owner = tile_cols // own_blocks
    slot_hits = (slot_owner[None, :] == owner_ids[:, None]) & (every_slot < live_count)[None, :]
    wanted = jnp.max(jnp.where(slot_hits, (tile_cols % own_blocks)[None, :], 0), axis=1)
    asked_blocks = lax.all_to_all(
        wanted.reshape(owners, 1), "blk", split_axis=0, concat_axis=0, tiled=True
    ).reshape(owners)

    own_scale = variant_scale.astype(jnp.float32)
    asked_scale = jnp.take(own_scale.reshape(own_blocks, edge), asked_blocks, axis=0)
    asked_sketch = jnp.take(sketch.reshape(own_blocks, edge, width), asked_blocks, axis=0)
    served = (asked_scale[:, :, None] * asked_sketch.astype(jnp.float32)).astype(jnp.bfloat16)
    fetched_sketch = lax.all_to_all(served, "blk", split_axis=0, concat_axis=0, tiled=True)

    panel = (owners, edge, width)
    group_terms = pl.pallas_call(
        range_kernel,
        out_shape=jax.ShapeDtypeStruct(panel, jnp.bfloat16),
        in_specs=[SMEM_SPEC] * 3 + [VMEM_SPEC] * 2,
        out_specs=VMEM_SPEC,
        scratch_shapes=[
            pltpu.VMEM((own_rows, edge, width), jnp.float32),
            pltpu.VMEM((own_rows, edge, width), jnp.bfloat16),
            pltpu.VMEM(panel, jnp.float32),
        ],
        compiler_params=PARAMS,
        name="range_terms",
    )(tile_rows, slot_owner, tile_count, tiles, fetched_sketch)
    arrived_terms = lax.all_to_all(group_terms, "blk", split_axis=0, concat_axis=0, tiled=True)
    squares = jnp.broadcast_to((asked_scale * asked_scale)[:, :, None], (owners, edge, edge))
    weighted = pl.pallas_call(
        weight_kernel,
        out_shape=jax.ShapeDtypeStruct(panel, jnp.bfloat16),
        in_specs=[SMEM_SPEC] + [VMEM_SPEC] * 2,
        out_specs=VMEM_SPEC,
        scratch_shapes=[pltpu.VMEM((own_blocks, edge, width), jnp.float32)],
        compiler_params=PARAMS,
        name="weighted_rows",
    )(asked_blocks, squares, arrived_terms)
    fetched_weighted = lax.all_to_all(weighted, "blk", split_axis=0, concat_axis=0, tiled=True)
    power_rows = pl.pallas_call(
        power_kernel,
        out_shape=jax.ShapeDtypeStruct((own_rows, edge, width), jnp.bfloat16),
        in_specs=[SMEM_SPEC] * 3 + [VMEM_SPEC] * 2,
        out_specs=VMEM_SPEC,
        scratch_shapes=[pltpu.VMEM((own_rows, edge, width), jnp.float32)],
        compiler_params=PARAMS,
        name="power_rows",
    )(tile_rows, slot_owner, tile_count, tiles, fetched_weighted)
    power_rows = power_rows.reshape(own_rows * edge, width)

    total_rows = own_rows * edge * owners
    partner_half = from_partner(power_rows, "col", 0)
    col_index = lax.axis_index("col")
    all_columns = jnp.where(
        col_index == 0,
        jnp.concatenate([power_rows, partner_half], axis=1),
        jnp.concatenate([partner_half, power_rows], axis=1),
    )
    gram_matrix = lax.psum(gram_of(all_columns), "blk") / total_rows
    size = gram_matrix.shape[0]
    return pl.pallas_call(
        basis_kernel,
        out_shape=jax.ShapeDtypeStruct((own_rows * edge, width), jnp.float32),
        in_specs=[SMEM_SPEC] + [VMEM_SPEC] * 2,
        out_specs=VMEM_SPEC,
        scratch_shapes=[pltpu.VMEM((size, size), jnp.float32)],
        compiler_params=PARAMS,
        name="basis_rows",
    )(col_index.reshape(1).astype(jnp.int32), gram_matrix, all_columns)


def solution(mesh):
    placed = (P("blk", None, None), P("blk"), P("blk"), P("blk"), P("blk", "col"), P("blk"))
    return jax.shard_map(
        local, mesh=mesh, in_specs=placed, out_specs=P("blk", "col"), check_vma=False
    )
```

```python
import functools
import jax
import jax.numpy as jnp
from jax import lax
from jax.experimental import pallas as pl
from jax.experimental.pallas import tpu as pltpu
from jax.sharding import PartitionSpec as P

TPR = 6
RB_DEV = 4
STEP = 3
PANEL = 8
VMEM_BYTES = 60 * 2**20
HIGHEST = lax.Precision.HIGHEST

SMEM_SPEC = pl.BlockSpec(memory_space=pltpu.SMEM)
VMEM_SPEC = pl.BlockSpec(memory_space=pltpu.VMEM)
PARAMS = pltpu.CompilerParams(vmem_limit_bytes=VMEM_BYTES)


def forward_rows(rows_ref, owner_ref, count, tiles_ref, fetched_ref, acc_ref):
    acc_ref[...] = jnp.zeros_like(acc_ref)

    def turn(index, carry):
        slots = [index * STEP + step for step in range(STEP)]
        products = [
            jnp.dot(
                tiles_ref[slot], fetched_ref[owner_ref[slot]], preferred_element_type=jnp.float32
            )
            for slot in slots
        ]
        for slot, product in zip(slots, products):
            acc_ref[rows_ref[slot]] += product
        return carry

    lax.fori_loop(0, count // STEP, turn, 0)


def range_kernel(rows_ref, owner_ref, count_ref, tiles_ref, fetched_ref, terms_ref, acc_ref, held_ref, sum_ref):
    count = count_ref[0]
    forward_rows(rows_ref, owner_ref, count, tiles_ref, fetched_ref, acc_ref)
    held_ref[...] = acc_ref[...].astype(jnp.bfloat16)
    sum_ref[...] = jnp.zeros_like(sum_ref)

    def turn(index, carry):
        slots = [index * STEP + step for step in range(STEP)]
        products = [
            lax.dot_general(
                tiles_ref[slot],
                held_ref[rows_ref[slot]],
                (((0,), (0,)), ((), ())),
                preferred_element_type=jnp.float32,
            )
            for slot in slots
        ]
        for slot, product in zip(slots, products):
            sum_ref[owner_ref[slot]] += product
        return carry

    lax.fori_loop(0, count // STEP, turn, 0)
    terms_ref[...] = sum_ref[...].astype(jnp.bfloat16)


def power_kernel(rows_ref, owner_ref, count_ref, tiles_ref, fetched_ref, out_ref, acc_ref):
    forward_rows(rows_ref, owner_ref, count_ref[0], tiles_ref, fetched_ref, acc_ref)
    out_ref[...] = acc_ref[...].astype(jnp.bfloat16)


def weight_kernel(asked_ref, square_ref, terms_ref, out_ref, sum_ref):
    owners, edge, width = terms_ref.shape

    def clear(q, carry):
        sum_ref[asked_ref[q]] = jnp.zeros((edge, width), jnp.float32)
        return carry

    def gather(q, carry):
        sum_ref[asked_ref[q]] += terms_ref[q].astype(jnp.float32)
        return carry

    def scale(q, carry):
        total = sum_ref[asked_ref[q]]
        for part in range(0, width, edge):
            out_ref[q, :, part : part + edge] = (
                square_ref[q] * total[:, part : part + edge]
            ).astype(jnp.bfloat16)
        return carry

    lax.fori_loop(0, owners, clear, 0)
    lax.fori_loop(0, owners, gather, 0)
    lax.fori_loop(0, owners, scale, 0)


def invert_block(block):
    edge = block.shape[0]
    lanes = lax.broadcasted_iota(jnp.int32, (PANEL, edge), 1)
    sublanes = lax.broadcasted_iota(jnp.int32, (PANEL, edge), 0)
    strips = [block[start : start + PANEL, :] for start in range(0, edge, PANEL)]
    done = []
    for panel in range(len(strips)):
        first = panel * PANEL
        live = strips[panel:]
        columns = [
            [
                jnp.broadcast_to(strip[:, first + k : first + k + 1], (PANEL, edge))
                for strip in live
            ]
            for k in range(PANEL)
        ]
        inside = (lanes >= first) & (lanes < first + PANEL)
        unit = (lanes == first + sublanes).astype(jnp.float32)
        live = [
            jnp.where(inside, unit if at == 0 else 0.0, strip) for at, strip in enumerate(live)
        ]
        pivots = jnp.ones((PANEL, edge), jnp.float32)
        for i in range(PANEL):
            pivot = jnp.broadcast_to(columns[i][0][i : i + 1, :], (PANEL, edge))
            pivots = jnp.where(sublanes == i, pivot, pivots)
            factor = 1.0 / pivot
            row = jnp.broadcast_to(live[0][i : i + 1, :], (PANEL, edge))
            heads = [
                jnp.broadcast_to(columns[k][0][i : i + 1, :], (PANEL, edge))
                for k in range(i + 1, PANEL)
            ]
            for at in range(len(live)):
                times = columns[i][at] * factor
                if at == 0:
                    times = jnp.where(sublanes > i, times, 0.0)
                live[at] = live[at] - times * row
                for k in range(i + 1, PANEL):
                    columns[k][at] = columns[k][at] - times * heads[k - i - 1]
        done.append(jnp.where(lanes <= first + sublanes, live[0] * lax.rsqrt(pivots), 0.0))
        strips = strips[: panel + 1] + live[1:]
    return jnp.concatenate(done, axis=0)


def basis_kernel(col_ref, blocks_ref, own_ref, other_ref, out_ref, held_ref):
    width = out_ref.shape[1]
    edge = blocks_ref.shape[2]
    half = width // edge
    size = 2 * width
    for block_row, block_col, holder, index in block_places(half):
        held_ref[
            block_row * edge : (block_row + 1) * edge, block_col * edge : (block_col + 1) * edge
        ] = blocks_ref[holder, index * edge : (index + 1) * edge, :]
    for start in range(0, size, edge):
        stop = start + edge
        inverse = invert_block(held_ref[start:stop, start:stop])
        if start:
            before = jnp.dot(
                inverse, held_ref[start:stop, :start],
                precision=HIGHEST, preferred_element_type=jnp.float32,
            )
            held_ref[start:stop, :start] = before
        held_ref[start:stop, start:stop] = inverse
        if stop < size:
            panel = lax.dot_general(
                held_ref[stop:, start:stop], inverse, (((1,), (1,)), ((), ())),
                precision=HIGHEST, preferred_element_type=jnp.float32,
            )
            held_ref[stop:, stop:] -= lax.dot_general(
                panel, panel, (((1,), (1,)), ((), ())),
                precision=HIGHEST, preferred_element_type=jnp.float32,
            )
            if start:
                held_ref[stop:, :start] -= jnp.dot(
                    panel, before, precision=HIGHEST, preferred_element_type=jnp.float32
                )
            held_ref[stop:, start:stop] = -jnp.dot(
                panel, inverse, precision=HIGHEST, preferred_element_type=jnp.float32
            )
            held_ref[start:stop, stop:] = jnp.zeros((edge, size - stop), jnp.float32)

    def add_half(rows_ref, first):
        own = held_ref[pl.ds(pl.multiple_of(col_ref[0] * width, width), width), first : first + width]
        high = own.astype(jnp.bfloat16)
        rest = own - high.astype(jnp.float32)
        middle = rest.astype(jnp.bfloat16)
        low = (rest - middle.astype(jnp.float32)).astype(jnp.bfloat16)
        total = jnp.zeros(out_ref.shape, jnp.float32)
        for piece in (low, middle, high):
            total += lax.dot_general(
                rows_ref[...], piece, (((1,), (1,)), ((), ())),
                preferred_element_type=jnp.float32,
            )
        return total

    @pl.when(col_ref[0] == 0)
    def _():
        out_ref[...] = add_half(own_ref, 0)

    @pl.when(col_ref[0] != 0)
    def _():
        out_ref[...] = add_half(other_ref, 0) + add_half(own_ref, width)


def block_places(half):
    places = []
    for holder in range(2):
        index = 0
        for block_col in range(half):
            for block_row in range(block_col, half):
                places.append((holder * half + block_row, holder * half + block_col, holder, index))
                index += 1
        for block_col in range(half // 2):
            for block_row in range(half):
                places.append(
                    (half + block_row, holder * (half // 2) + block_col, holder, index)
                )
                index += 1
    return places


def gram_kernel(
    owners, total_rows, chunk, own_ref, other_ref, blocks_ref,
    part_ref, inbox_ref, pair_sems, part_send, part_recv, sum_send, sum_recv, pass_send, pass_recv,
):
    me = lax.axis_index("blk")
    col = lax.axis_index("col")
    partner = {"blk": me, "col": 1 - col}
    width = own_ref.shape[1]
    edge = blocks_ref.shape[2]
    half = width // edge
    own_depth = edge * half * (half + 1) // 2
    depth = edge * (half * (half + 1) // 2 + half * half // 2)
    reducers = (depth + chunk - 1) // chunk
    early = own_depth // chunk

    barrier = pltpu.get_barrier_semaphore()

    def greet(d, carry):
        pl.semaphore_signal(
            barrier, inc=1, device_id={"blk": lax.rem(me + d, owners), "col": col},
            device_id_type=pl.DeviceIdType.MESH,
        )
        return carry

    lax.fori_loop(1, owners, greet, 0)
    pl.semaphore_signal(barrier, inc=1, device_id=partner, device_id_type=pl.DeviceIdType.MESH)
    pl.semaphore_wait(barrier, owners)

    def rows_of(q):
        return pl.ds(pl.multiple_of(q * chunk, chunk), chunk)

    def remote(src, dst, send_sem, recv_sem, device):
        return pltpu.make_async_remote_copy(
            src_ref=src, dst_ref=dst, send_sem=send_sem, recv_sem=recv_sem,
            device_id=device, device_id_type=pl.DeviceIdType.MESH,
        )

    def peer(q):
        return {"blk": q, "col": col}

    def part_copy(src, q):
        return remote(
            part_ref.at[rows_of(q)], inbox_ref.at[src], part_send.at[q], part_recv.at[src], peer(q)
        )

    def sum_copy(src, q):
        rows = blocks_ref.at[col, rows_of(src)]
        return remote(rows, rows, sum_send.at[q], sum_recv.at[src], peer(q))

    def pass_copy(holder, q):
        rows = blocks_ref.at[holder, rows_of(q)]
        return remote(rows, rows, pass_send.at[q], pass_recv.at[q], partner)

    def each_peer(step, low, high):
        def turn(d, carry):
            q = lax.rem(me + d, owners)

            @pl.when((q >= low) & (q < high))
            def _():
                step(q)

            return carry

        lax.fori_loop(1, owners, turn, 0)

    pair = remote(own_ref, other_ref, pair_sems.at[0], pair_sems.at[1], partner)
    pair.start()

    own = own_ref[...]
    own_gram = lax.dot_general(
        own, own, (((0,), (0,)), ((), ())), preferred_element_type=jnp.float32
    )
    index = 0
    for block_col in range(half):
        for block_row in range(block_col, half):
            part_ref[index * edge : (index + 1) * edge, :] = own_gram[
                block_row * edge : (block_row + 1) * edge, block_col * edge : (block_col + 1) * edge
            ]
            index += 1
    each_peer(lambda q: part_copy(me, q).start(), 0, early)

    pair.wait()
    other = other_ref[...]
    low_half = jnp.where(col == 0, own, other)
    high_half = jnp.where(col == 0, other, own)
    span = width // 2
    low_part = jnp.where(col == 0, low_half[:, :span], low_half[:, span:])
    cross = lax.dot_general(
        high_half, low_part, (((0,), (0,)), ((), ())), preferred_element_type=jnp.float32
    )
    for block_col in range(half // 2):
        for block_row in range(half):
            part_ref[index * edge : (index + 1) * edge, :] = cross[
                block_row * edge : (block_row + 1) * edge, block_col * edge : (block_col + 1) * edge
            ]
            index += 1
    each_peer(lambda q: part_copy(me, q).start(), early, reducers)

    @pl.when(me < reducers)
    def _():
        def add(d, total):
            src = lax.rem(me + owners - d, owners)
            part_copy(src, me).wait_recv()
            return total + inbox_ref[src]

        total = lax.fori_loop(1, owners, add, part_ref[rows_of(me)])
        blocks_ref[col, rows_of(me)] = total / total_rows

        def send(d, carry):
            sum_copy(me, lax.rem(me + d, owners)).start()
            return carry

        lax.fori_loop(1, owners, send, 0)
        pass_copy(col, me).start()

    def hand_on(d, carry):
        src = lax.rem(me + owners - d, owners)

        @pl.when(src < reducers)
        def _():
            sum_copy(src, src).wait_recv()
            pass_copy(col, src).start()

        return carry

    lax.fori_loop(1, owners, hand_on, 0)

    def finish(q, carry):
        pass_copy(1 - col, q).wait_recv()
        pass_copy(col, q).wait_send()
        return carry

    lax.fori_loop(0, reducers, finish, 0)
    each_peer(lambda q: part_copy(me, q).wait_send(), 0, reducers)

    @pl.when(me < reducers)
    def _():
        each_peer(lambda q: sum_copy(me, q).wait_send(), 0, owners)


def local(tiles, tile_rows, tile_cols, tile_count, sketch, variant_scale):
    width = sketch.shape[1]
    edge = tiles.shape[1]
    owners = lax.axis_size("blk")
    own_blocks = sketch.shape[0] // edge
    own_rows = RB_DEV
    live_count = tile_count[0]
    every_slot = jnp.arange(tiles.shape[0], dtype=jnp.int32)
    owner_ids = jnp.arange(owners, dtype=jnp.int32)
    slot_owner = tile_cols // own_blocks
    slot_hits = (slot_owner[None, :] == owner_ids[:, None]) & (every_slot < live_count)[None, :]
    wanted = jnp.max(jnp.where(slot_hits, (tile_cols % own_blocks)[None, :], 0), axis=1)
    asked_blocks = lax.all_to_all(
        wanted.reshape(owners, 1), "blk", split_axis=0, concat_axis=0, tiled=True
    ).reshape(owners)

    own_scale = variant_scale.astype(jnp.float32)
    asked_scale = jnp.take(own_scale.reshape(own_blocks, edge), asked_blocks, axis=0)
    asked_sketch = jnp.take(sketch.reshape(own_blocks, edge, width), asked_blocks, axis=0)
    served = (asked_scale[:, :, None] * asked_sketch.astype(jnp.float32)).astype(jnp.bfloat16)
    fetched_sketch = lax.all_to_all(served, "blk", split_axis=0, concat_axis=0, tiled=True)

    panel = (owners, edge, width)
    group_terms = pl.pallas_call(
        range_kernel,
        out_shape=jax.ShapeDtypeStruct(panel, jnp.bfloat16),
        in_specs=[SMEM_SPEC] * 3 + [VMEM_SPEC] * 2,
        out_specs=VMEM_SPEC,
        scratch_shapes=[
            pltpu.VMEM((own_rows, edge, width), jnp.float32),
            pltpu.VMEM((own_rows, edge, width), jnp.bfloat16),
            pltpu.VMEM(panel, jnp.float32),
        ],
        compiler_params=PARAMS,
        name="range_terms",
    )(tile_rows, slot_owner, tile_count, tiles, fetched_sketch)
    arrived_terms = lax.all_to_all(group_terms, "blk", split_axis=0, concat_axis=0, tiled=True)
    squares = jnp.broadcast_to((asked_scale * asked_scale)[:, :, None], (owners, edge, edge))
    weighted = pl.pallas_call(
        weight_kernel,
        out_shape=jax.ShapeDtypeStruct(panel, jnp.bfloat16),
        in_specs=[SMEM_SPEC] + [VMEM_SPEC] * 2,
        out_specs=VMEM_SPEC,
        scratch_shapes=[pltpu.VMEM((own_blocks, edge, width), jnp.float32)],
        compiler_params=PARAMS,
        name="weighted_rows",
    )(asked_blocks, squares, arrived_terms)
    fetched_weighted = lax.all_to_all(weighted, "blk", split_axis=0, concat_axis=0, tiled=True)
    power_rows = pl.pallas_call(
        power_kernel,
        out_shape=jax.ShapeDtypeStruct((own_rows, edge, width), jnp.bfloat16),
        in_specs=[SMEM_SPEC] * 3 + [VMEM_SPEC] * 2,
        out_specs=VMEM_SPEC,
        scratch_shapes=[pltpu.VMEM((own_rows, edge, width), jnp.float32)],
        compiler_params=PARAMS,
        name="power_rows",
    )(tile_rows, slot_owner, tile_count, tiles, fetched_weighted)
    power_rows = power_rows.reshape(own_rows * edge, width)

    total_rows = own_rows * edge * owners
    half = width // edge
    depth = edge * (half * (half + 1) // 2 + half * half // 2)
    chunk = -(-depth // (8 * owners)) * 8
    reducers = -(-depth // chunk)
    other_rows, blocks = pl.pallas_call(
        functools.partial(gram_kernel, owners, total_rows, chunk),
        out_shape=(
            jax.ShapeDtypeStruct(power_rows.shape, jnp.bfloat16),
            jax.ShapeDtypeStruct((2, reducers * chunk, edge), jnp.float32),
        ),
        in_specs=[VMEM_SPEC],
        out_specs=(VMEM_SPEC, VMEM_SPEC),
        scratch_shapes=[
            pltpu.VMEM((reducers * chunk, edge), jnp.float32),
            pltpu.VMEM((owners, chunk, edge), jnp.float32),
            pltpu.SemaphoreType.DMA((2,)),
        ]
        + [pltpu.SemaphoreType.DMA((owners,))] * 6,
        compiler_params=pltpu.CompilerParams(
            vmem_limit_bytes=VMEM_BYTES, collective_id=0, has_side_effects=True
        ),
        name="gram_blocks",
    )(power_rows)
    return pl.pallas_call(
        basis_kernel,
        out_shape=jax.ShapeDtypeStruct((own_rows * edge, width), jnp.float32),
        in_specs=[SMEM_SPEC] + [VMEM_SPEC] * 3,
        out_specs=VMEM_SPEC,
        scratch_shapes=[pltpu.VMEM((2 * width, 2 * width), jnp.float32)],
        compiler_params=PARAMS,
        name="basis_rows",
    )(lax.axis_index("col").reshape(1).astype(jnp.int32), blocks, power_rows, other_rows)


def solution(mesh):
    placed = (P("blk", None, None), P("blk"), P("blk"), P("blk"), P("blk", "col"), P("blk"))
    return jax.shard_map(
        local, mesh=mesh, in_specs=placed, out_specs=P("blk", "col"), check_vma=False
    )
```

```python
import functools
import jax
import jax.numpy as jnp
from jax import lax
from jax.experimental import pallas as pl
from jax.experimental.pallas import tpu as pltpu
from jax.sharding import PartitionSpec as P

TPR = 6
RB_DEV = 4
PANEL = 8
VMEM_BYTES = 60 * 2**20
HIGHEST = lax.Precision.HIGHEST

SMEM_SPEC = pl.BlockSpec(memory_space=pltpu.SMEM)
VMEM_SPEC = pl.BlockSpec(memory_space=pltpu.VMEM)
PARAMS = pltpu.CompilerParams(vmem_limit_bytes=VMEM_BYTES)


def exchange_kernel(
    owners, slot_ref, wanted_ref, scale_ref, tiles_ref, sketch_ref, rows_ref,
    asked_in, asked, tile_set, send, fetched, arrived, sums, squares, acc, held,
    ask_sems, sketch_sems, term_sems, weight_sems, local_sem,
):
    me = lax.axis_index("blk")
    col = lax.axis_index("col")
    slots, edge, _ = tiles_ref.shape
    width = sketch_ref.shape[2]
    own_rows = acc.shape[0] // edge

    barrier = pltpu.get_barrier_semaphore()

    def each(step, first=1):
        def turn(d, carry):
            step(d)
            return carry

        lax.fori_loop(first, owners, turn, 0)

    def ahead(d):
        return lax.rem(me + d, owners)

    def behind(d):
        return lax.rem(me + owners - d, owners)

    def greet(d):
        pl.semaphore_signal(
            barrier, inc=1, device_id={"blk": ahead(d), "col": col},
            device_id_type=pl.DeviceIdType.MESH,
        )

    each(greet)

    def copy_of(source, target, sems):
        def make(src, q):
            return pltpu.make_async_remote_copy(
                src_ref=source.at[q], dst_ref=target.at[src],
                send_sem=sems.at[0, q], recv_sem=sems.at[1, src],
                device_id={"blk": q, "col": col}, device_id_type=pl.DeviceIdType.MESH,
            )

        return make

    ask_copy = copy_of(wanted_ref, asked_in, ask_sems)
    sketch_copy = copy_of(send, fetched, sketch_sems)
    term_copy = copy_of(send, arrived, term_sems)
    weight_copy = copy_of(send, fetched, weight_sems)

    tile_set[:slots] = tiles_ref[...]
    tile_set[slots] = jnp.zeros((edge, edge), jnp.bfloat16)
    asked_in[me] = wanted_ref[me]
    pl.semaphore_wait(barrier, owners - 1)
    each(lambda d: ask_copy(me, ahead(d)).start())
    each(lambda d: ask_copy(behind(d), me).wait_recv())
    into_scalars = pltpu.make_async_copy(asked_in, asked, local_sem)
    into_scalars.start()
    into_scalars.wait()

    lanes = lax.broadcasted_iota(jnp.int32, (edge, edge), 1)
    sublanes = lax.broadcasted_iota(jnp.int32, (edge, edge), 0)
    ones = jnp.ones((edge, edge), jnp.bfloat16)

    def served(q):
        block = asked[q, 0, 0]
        spread = jnp.broadcast_to(scale_ref[block], (edge, edge))
        diagonal = jnp.where(lanes == sublanes, spread, 0.0).astype(jnp.bfloat16)
        column = jnp.dot(diagonal, ones, preferred_element_type=jnp.float32)
        squares[q] = column * column
        rows = sketch_ref[block].astype(jnp.float32)
        return (rows * jnp.concatenate([column] * (width // edge), axis=1)).astype(jnp.bfloat16)

    def serve(d):
        q = ahead(d)
        send[q] = served(q)
        sketch_copy(me, q).start()

    each(serve)
    fetched[me] = served(me)

    def stack_of(owner):
        return jnp.concatenate(
            [tile_set[slot_ref[owner * own_rows + row]] for row in range(own_rows)], axis=0
        )

    def forward(copies):
        acc[...] = jnp.dot(stack_of(me), fetched[me], preferred_element_type=jnp.float32)

        def take(d):
            owner = behind(d)
            copies(owner, me).wait_recv()
            acc[...] += jnp.dot(
                stack_of(owner), fetched[owner], preferred_element_type=jnp.float32
            )

        each(take)

    forward(sketch_copy)
    held[...] = acc[...].astype(jnp.bfloat16)
    each(lambda d: sketch_copy(me, ahead(d)).wait_send())

    def term_of(owner):
        return lax.dot_general(
            stack_of(owner), held[...], (((0,), (0,)), ((), ())),
            preferred_element_type=jnp.float32,
        ).astype(jnp.bfloat16)

    def give(d):
        q = ahead(d)
        send[q] = term_of(q)
        term_copy(me, q).start()

    each(give)
    arrived[me] = term_of(me)

    def share(src, q):
        same = (asked[src, 0, 0] == asked[q, 0, 0]).astype(jnp.float32)
        return same * arrived[src].astype(jnp.float32)

    def begin(q, carry):
        sums[q] = share(me, q)
        return carry

    lax.fori_loop(0, owners, begin, 0)

    def gather(d):
        src = behind(d)
        term_copy(src, me).wait_recv()

        def add(q, carry):
            sums[q] += share(src, q)
            return carry

        lax.fori_loop(0, owners, add, 0)

    each(gather)
    each(lambda d: term_copy(me, ahead(d)).wait_send())

    def weighted(q):
        square = jnp.concatenate([squares[q]] * (width // edge), axis=1)
        return (square * sums[q]).astype(jnp.bfloat16)

    def give_weighted(d):
        q = ahead(d)
        send[q] = weighted(q)
        weight_copy(me, q).start()

    each(give_weighted)
    fetched[me] = weighted(me)
    forward(weight_copy)
    rows_ref[...] = acc[...].astype(jnp.bfloat16)
    each(lambda d: ask_copy(me, ahead(d)).wait_send())
    each(lambda d: weight_copy(me, ahead(d)).wait_send())


def invert_block(block):
    edge = block.shape[0]
    lanes = lax.broadcasted_iota(jnp.int32, (PANEL, edge), 1)
    sublanes = lax.broadcasted_iota(jnp.int32, (PANEL, edge), 0)
    strips = [block[start : start + PANEL, :] for start in range(0, edge, PANEL)]
    done = []
    for panel in range(len(strips)):
        first = panel * PANEL
        live = strips[panel:]
        columns = [
            [
                jnp.broadcast_to(strip[:, first + k : first + k + 1], (PANEL, edge))
                for strip in live
            ]
            for k in range(PANEL)
        ]
        inside = (lanes >= first) & (lanes < first + PANEL)
        unit = (lanes == first + sublanes).astype(jnp.float32)
        live = [
            jnp.where(inside, unit if at == 0 else 0.0, strip) for at, strip in enumerate(live)
        ]
        pivots = jnp.ones((PANEL, edge), jnp.float32)
        for i in range(PANEL):
            pivot = jnp.broadcast_to(columns[i][0][i : i + 1, :], (PANEL, edge))
            pivots = jnp.where(sublanes == i, pivot, pivots)
            factor = 1.0 / pivot
            row = jnp.broadcast_to(live[0][i : i + 1, :], (PANEL, edge))
            heads = [
                jnp.broadcast_to(columns[k][0][i : i + 1, :], (PANEL, edge))
                for k in range(i + 1, PANEL)
            ]
            for at in range(len(live)):
                times = columns[i][at] * factor
                if at == 0:
                    times = jnp.where(sublanes > i, times, 0.0)
                live[at] = live[at] - times * row
                for k in range(i + 1, PANEL):
                    columns[k][at] = columns[k][at] - times * heads[k - i - 1]
        done.append(jnp.where(lanes <= first + sublanes, live[0] * lax.rsqrt(pivots), 0.0))
        strips = strips[: panel + 1] + live[1:]
    return jnp.concatenate(done, axis=0)


def basis_kernel(col_ref, blocks_ref, own_ref, other_ref, out_ref, held_ref):
    width = out_ref.shape[1]
    edge = blocks_ref.shape[2]
    half = width // edge
    size = 2 * width
    for block_row, block_col, holder, index in block_places(half):
        held_ref[
            block_row * edge : (block_row + 1) * edge, block_col * edge : (block_col + 1) * edge
        ] = blocks_ref[holder, index * edge : (index + 1) * edge, :]
    for start in range(0, size, edge):
        stop = start + edge
        inverse = invert_block(held_ref[start:stop, start:stop])
        if start:
            before = jnp.dot(
                inverse, held_ref[start:stop, :start],
                precision=HIGHEST, preferred_element_type=jnp.float32,
            )
            held_ref[start:stop, :start] = before
        held_ref[start:stop, start:stop] = inverse
        if stop < size:
            panel = lax.dot_general(
                held_ref[stop:, start:stop], inverse, (((1,), (1,)), ((), ())),
                precision=HIGHEST, preferred_element_type=jnp.float32,
            )
            held_ref[stop:, stop:] -= lax.dot_general(
                panel, panel, (((1,), (1,)), ((), ())),
                precision=HIGHEST, preferred_element_type=jnp.float32,
            )
            if start:
                held_ref[stop:, :start] -= jnp.dot(
                    panel, before, precision=HIGHEST, preferred_element_type=jnp.float32
                )
            held_ref[stop:, start:stop] = -jnp.dot(
                panel, inverse, precision=HIGHEST, preferred_element_type=jnp.float32
            )
            held_ref[start:stop, stop:] = jnp.zeros((edge, size - stop), jnp.float32)

    def add_half(rows_ref, first):
        own = held_ref[pl.ds(pl.multiple_of(col_ref[0] * width, width), width), first : first + width]
        high = own.astype(jnp.bfloat16)
        rest = own - high.astype(jnp.float32)
        middle = rest.astype(jnp.bfloat16)
        low = (rest - middle.astype(jnp.float32)).astype(jnp.bfloat16)
        total = jnp.zeros(out_ref.shape, jnp.float32)
        for piece in (low, middle, high):
            total += lax.dot_general(
                rows_ref[...], piece, (((1,), (1,)), ((), ())),
                preferred_element_type=jnp.float32,
            )
        return total

    @pl.when(col_ref[0] == 0)
    def _():
        out_ref[...] = add_half(own_ref, 0)

    @pl.when(col_ref[0] != 0)
    def _():
        out_ref[...] = add_half(other_ref, 0) + add_half(own_ref, width)


def block_places(half):
    places = []
    for holder in range(2):
        index = 0
        for block_col in range(half):
            for block_row in range(block_col, half):
                places.append((holder * half + block_row, holder * half + block_col, holder, index))
                index += 1
        for block_col in range(half // 2):
            for block_row in range(half):
                places.append(
                    (half + block_row, holder * (half // 2) + block_col, holder, index)
                )
                index += 1
    return places


def gram_kernel(
    owners, total_rows, chunk, own_ref, other_ref, blocks_ref,
    part_ref, inbox_ref, pair_sems, part_send, part_recv, sum_send, sum_recv, pass_send, pass_recv,
):
    me = lax.axis_index("blk")
    col = lax.axis_index("col")
    partner = {"blk": me, "col": 1 - col}
    width = own_ref.shape[1]
    edge = blocks_ref.shape[2]
    half = width // edge
    own_depth = edge * half * (half + 1) // 2
    depth = edge * (half * (half + 1) // 2 + half * half // 2)
    reducers = (depth + chunk - 1) // chunk
    early = own_depth // chunk

    barrier = pltpu.get_barrier_semaphore()

    def greet(d, carry):
        pl.semaphore_signal(
            barrier, inc=1, device_id={"blk": lax.rem(me + d, owners), "col": col},
            device_id_type=pl.DeviceIdType.MESH,
        )
        return carry

    lax.fori_loop(1, owners, greet, 0)
    pl.semaphore_signal(barrier, inc=1, device_id=partner, device_id_type=pl.DeviceIdType.MESH)
    pl.semaphore_wait(barrier, owners)

    def rows_of(q):
        return pl.ds(pl.multiple_of(q * chunk, chunk), chunk)

    def remote(src, dst, send_sem, recv_sem, device):
        return pltpu.make_async_remote_copy(
            src_ref=src, dst_ref=dst, send_sem=send_sem, recv_sem=recv_sem,
            device_id=device, device_id_type=pl.DeviceIdType.MESH,
        )

    def peer(q):
        return {"blk": q, "col": col}

    def part_copy(src, q):
        return remote(
            part_ref.at[rows_of(q)], inbox_ref.at[src], part_send.at[q], part_recv.at[src], peer(q)
        )

    def sum_copy(src, q):
        rows = blocks_ref.at[col, rows_of(src)]
        return remote(rows, rows, sum_send.at[q], sum_recv.at[src], peer(q))

    def pass_copy(holder, q):
        rows = blocks_ref.at[holder, rows_of(q)]
        return remote(rows, rows, pass_send.at[q], pass_recv.at[q], partner)

    def each_peer(step, low, high):
        def turn(d, carry):
            q = lax.rem(me + d, owners)

            @pl.when((q >= low) & (q < high))
            def _():
                step(q)

            return carry

        lax.fori_loop(1, owners, turn, 0)

    pair = remote(own_ref, other_ref, pair_sems.at[0], pair_sems.at[1], partner)
    pair.start()

    own = own_ref[...]
    own_gram = lax.dot_general(
        own, own, (((0,), (0,)), ((), ())), preferred_element_type=jnp.float32
    )
    index = 0
    for block_col in range(half):
        for block_row in range(block_col, half):
            part_ref[index * edge : (index + 1) * edge, :] = own_gram[
                block_row * edge : (block_row + 1) * edge, block_col * edge : (block_col + 1) * edge
            ]
            index += 1
    each_peer(lambda q: part_copy(me, q).start(), 0, early)

    pair.wait()
    other = other_ref[...]
    low_half = jnp.where(col == 0, own, other)
    high_half = jnp.where(col == 0, other, own)
    span = width // 2
    low_part = jnp.where(col == 0, low_half[:, :span], low_half[:, span:])
    cross = lax.dot_general(
        high_half, low_part, (((0,), (0,)), ((), ())), preferred_element_type=jnp.float32
    )
    for block_col in range(half // 2):
        for block_row in range(half):
            part_ref[index * edge : (index + 1) * edge, :] = cross[
                block_row * edge : (block_row + 1) * edge, block_col * edge : (block_col + 1) * edge
            ]
            index += 1
    each_peer(lambda q: part_copy(me, q).start(), early, reducers)

    @pl.when(me < reducers)
    def _():
        def add(d, total):
            src = lax.rem(me + owners - d, owners)
            part_copy(src, me).wait_recv()
            return total + inbox_ref[src]

        total = lax.fori_loop(1, owners, add, part_ref[rows_of(me)])
        blocks_ref[col, rows_of(me)] = total / total_rows

        def send(d, carry):
            sum_copy(me, lax.rem(me + d, owners)).start()
            return carry

        lax.fori_loop(1, owners, send, 0)
        pass_copy(col, me).start()

    def hand_on(d, carry):
        src = lax.rem(me + owners - d, owners)

        @pl.when(src < reducers)
        def _():
            sum_copy(src, src).wait_recv()
            pass_copy(col, src).start()

        return carry

    lax.fori_loop(1, owners, hand_on, 0)

    def finish(q, carry):
        pass_copy(1 - col, q).wait_recv()
        pass_copy(col, q).wait_send()
        return carry

    lax.fori_loop(0, reducers, finish, 0)
    each_peer(lambda q: part_copy(me, q).wait_send(), 0, reducers)

    @pl.when(me < reducers)
    def _():
        each_peer(lambda q: sum_copy(me, q).wait_send(), 0, owners)


def local(tiles, tile_rows, tile_cols, tile_count, sketch, variant_scale):
    width = sketch.shape[1]
    edge = tiles.shape[1]
    owners = lax.axis_size("blk")
    own_blocks = sketch.shape[0] // edge
    own_rows = RB_DEV
    slots = tiles.shape[0]
    every_slot = jnp.arange(slots, dtype=jnp.int32)
    owner_ids = jnp.arange(owners, dtype=jnp.int32)
    live = every_slot < tile_count[0]
    slot_owner = tile_cols // own_blocks
    slot_hits = (slot_owner[None, :] == owner_ids[:, None]) & live[None, :]
    wanted = jnp.max(jnp.where(slot_hits, (tile_cols % own_blocks)[None, :], 0), axis=1)
    places = jnp.arange(owners * own_rows, dtype=jnp.int32)
    place_hits = ((slot_owner * own_rows + tile_rows)[None, :] == places[:, None]) & live[None, :]
    slot_of = jnp.min(jnp.where(place_hits, every_slot[None, :], slots), axis=1)
    panel = (owners, edge, width)
    power_rows = pl.pallas_call(
        functools.partial(exchange_kernel, owners),
        out_shape=jax.ShapeDtypeStruct((own_rows * edge, width), jnp.bfloat16),
        in_specs=[SMEM_SPEC] + [VMEM_SPEC] * 4,
        out_specs=VMEM_SPEC,
        scratch_shapes=[
            pltpu.VMEM((owners, 1, edge), jnp.int32),
            pltpu.SMEM((owners, 1, edge), jnp.int32),
            pltpu.VMEM((slots + 1, edge, edge), jnp.bfloat16),
            pltpu.VMEM(panel, jnp.bfloat16),
            pltpu.VMEM(panel, jnp.bfloat16),
            pltpu.VMEM(panel, jnp.bfloat16),
            pltpu.VMEM(panel, jnp.float32),
            pltpu.VMEM((owners, edge, edge), jnp.float32),
            pltpu.VMEM((own_rows * edge, width), jnp.float32),
            pltpu.VMEM((own_rows * edge, width), jnp.bfloat16),
        ]
        + [pltpu.SemaphoreType.DMA((2, owners))] * 4
        + [pltpu.SemaphoreType.DMA],
        compiler_params=pltpu.CompilerParams(
            vmem_limit_bytes=VMEM_BYTES, collective_id=1, has_side_effects=True
        ),
        name="exchange_rows",
    )(
        slot_of,
        jnp.broadcast_to(wanted[:, None, None], (owners, 1, edge)),
        variant_scale.astype(jnp.float32).reshape(own_blocks, 1, edge),
        tiles,
        sketch.reshape(own_blocks, edge, width),
    )

    total_rows = own_rows * edge * owners
    half = width // edge
    depth = edge * (half * (half + 1) // 2 + half * half // 2)
    chunk = -(-depth // (8 * owners)) * 8
    reducers = -(-depth // chunk)
    other_rows, blocks = pl.pallas_call(
        functools.partial(gram_kernel, owners, total_rows, chunk),
        out_shape=(
            jax.ShapeDtypeStruct(power_rows.shape, jnp.bfloat16),
            jax.ShapeDtypeStruct((2, reducers * chunk, edge), jnp.float32),
        ),
        in_specs=[VMEM_SPEC],
        out_specs=(VMEM_SPEC, VMEM_SPEC),
        scratch_shapes=[
            pltpu.VMEM((reducers * chunk, edge), jnp.float32),
            pltpu.VMEM((owners, chunk, edge), jnp.float32),
            pltpu.SemaphoreType.DMA((2,)),
        ]
        + [pltpu.SemaphoreType.DMA((owners,))] * 6,
        compiler_params=pltpu.CompilerParams(
            vmem_limit_bytes=VMEM_BYTES, collective_id=0, has_side_effects=True
        ),
        name="gram_blocks",
    )(power_rows)
    return pl.pallas_call(
        basis_kernel,
        out_shape=jax.ShapeDtypeStruct((own_rows * edge, width), jnp.float32),
        in_specs=[SMEM_SPEC] + [VMEM_SPEC] * 3,
        out_specs=VMEM_SPEC,
        scratch_shapes=[pltpu.VMEM((2 * width, 2 * width), jnp.float32)],
        compiler_params=PARAMS,
        name="basis_rows",
    )(lax.axis_index("col").reshape(1).astype(jnp.int32), blocks, power_rows, other_rows)


def solution(mesh):
    placed = (P("blk", None, None), P("blk"), P("blk"), P("blk"), P("blk", "col"), P("blk"))
    return jax.shard_map(
        local, mesh=mesh, in_specs=placed, out_specs=P("blk", "col"), check_vma=False
    )
```

```python
import functools
import jax
import jax.numpy as jnp
from jax import lax
from jax.experimental import pallas as pl
from jax.experimental.pallas import tpu as pltpu
from jax.sharding import PartitionSpec as P

TPR = 6
RB_DEV = 4
PANEL = 8
VMEM_BYTES = 60 * 2**20
HIGHEST = lax.Precision.HIGHEST

SMEM_SPEC = pl.BlockSpec(memory_space=pltpu.SMEM)
VMEM_SPEC = pl.BlockSpec(memory_space=pltpu.VMEM)
PARAMS = pltpu.CompilerParams(vmem_limit_bytes=VMEM_BYTES)


def exchange_kernel(
    owners, slot_ref, wanted_ref, scale_ref, tiles_ref, sketch_ref, rows_ref,
    asked_in, asked, tile_set, send, fetched, arrived, sums, squares, acc, held,
    ask_sems, sketch_sems, term_sems, weight_sems, local_sem,
):
    me = lax.axis_index("blk")
    col = lax.axis_index("col")
    slots, edge, _ = tiles_ref.shape
    width = sketch_ref.shape[2]
    own_rows = acc.shape[0] // edge

    barrier = pltpu.get_barrier_semaphore()

    def each(step, first=1):
        def turn(d, carry):
            step(d)
            return carry

        lax.fori_loop(first, owners, turn, 0)

    def ahead(d):
        return lax.rem(me + d, owners)

    def behind(d):
        return lax.rem(me + owners - d, owners)

    def greet(d):
        pl.semaphore_signal(
            barrier, inc=1, device_id={"blk": ahead(d), "col": col},
            device_id_type=pl.DeviceIdType.MESH,
        )

    each(greet)

    def copy_of(source, target, sems):
        def make(src, q):
            return pltpu.make_async_remote_copy(
                src_ref=source.at[q], dst_ref=target.at[src],
                send_sem=sems.at[0, q], recv_sem=sems.at[1, src],
                device_id={"blk": q, "col": col}, device_id_type=pl.DeviceIdType.MESH,
            )

        return make

    ask_copy = copy_of(wanted_ref, asked_in, ask_sems)
    sketch_copy = copy_of(send, fetched, sketch_sems)
    term_copy = copy_of(send, arrived, term_sems)
    weight_copy = copy_of(send, fetched, weight_sems)

    tile_set[:slots] = tiles_ref[...]
    tile_set[slots] = jnp.zeros((edge, edge), jnp.bfloat16)
    asked_in[me] = wanted_ref[me]
    pl.semaphore_wait(barrier, owners - 1)
    each(lambda d: ask_copy(me, ahead(d)).start())
    each(lambda d: ask_copy(behind(d), me).wait_recv())
    into_scalars = pltpu.make_async_copy(asked_in, asked, local_sem)
    into_scalars.start()
    into_scalars.wait()

    lanes = lax.broadcasted_iota(jnp.int32, (edge, edge), 1)
    sublanes = lax.broadcasted_iota(jnp.int32, (edge, edge), 0)
    ones = jnp.ones((edge, edge), jnp.bfloat16)

    def served(q):
        block = asked[q, 0, 0]
        spread = jnp.broadcast_to(scale_ref[block], (edge, edge))
        diagonal = jnp.where(lanes == sublanes, spread, 0.0).astype(jnp.bfloat16)
        column = jnp.dot(diagonal, ones, preferred_element_type=jnp.float32)
        squares[q] = column * column
        rows = sketch_ref[block].astype(jnp.float32)
        return (rows * jnp.concatenate([column] * (width // edge), axis=1)).astype(jnp.bfloat16)

    def serve(d):
        q = ahead(d)
        send[q] = served(q)
        sketch_copy(me, q).start()

    each(serve)
    fetched[me] = served(me)

    def stack_of(owner):
        return jnp.concatenate(
            [tile_set[slot_ref[owner * own_rows + row]] for row in range(own_rows)], axis=0
        )

    def forward(copies):
        acc[...] = jnp.dot(stack_of(me), fetched[me], preferred_element_type=jnp.float32)

        def take(d):
            owner = behind(d)
            copies(owner, me).wait_recv()
            acc[...] += jnp.dot(
                stack_of(owner), fetched[owner], preferred_element_type=jnp.float32
            )

        each(take)

    forward(sketch_copy)
    held[...] = acc[...].astype(jnp.bfloat16)
    each(lambda d: sketch_copy(me, ahead(d)).wait_send())

    def term_of(owner):
        return lax.dot_general(
            stack_of(owner), held[...], (((0,), (0,)), ((), ())),
            preferred_element_type=jnp.float32,
        ).astype(jnp.bfloat16)

    def give(d):
        q = ahead(d)
        send[q] = term_of(q)
        term_copy(me, q).start()

    each(give)
    arrived[me] = term_of(me)

    def share(src, q):
        same = (asked[src, 0, 0] == asked[q, 0, 0]).astype(jnp.float32)
        return same * arrived[src].astype(jnp.float32)

    def begin(q, carry):
        sums[q] = share(me, q)
        return carry

    lax.fori_loop(0, owners, begin, 0)

    def gather(d):
        src = behind(d)
        term_copy(src, me).wait_recv()

        def add(q, carry):
            sums[q] += share(src, q)
            return carry

        lax.fori_loop(0, owners, add, 0)

    each(gather)
    each(lambda d: term_copy(me, ahead(d)).wait_send())

    def weighted(q):
        square = jnp.concatenate([squares[q]] * (width // edge), axis=1)
        return (square * sums[q]).astype(jnp.bfloat16)

    def give_weighted(d):
        q = ahead(d)
        send[q] = weighted(q)
        weight_copy(me, q).start()

    each(give_weighted)
    fetched[me] = weighted(me)
    forward(weight_copy)
    rows_ref[...] = acc[...].astype(jnp.bfloat16)
    each(lambda d: ask_copy(me, ahead(d)).wait_send())
    each(lambda d: weight_copy(me, ahead(d)).wait_send())


def invert_block(block):
    edge = block.shape[0]
    lanes = lax.broadcasted_iota(jnp.int32, (PANEL, edge), 1)
    sublanes = lax.broadcasted_iota(jnp.int32, (PANEL, edge), 0)
    strips = [block[start : start + PANEL, :] for start in range(0, edge, PANEL)]
    done = []
    for panel in range(len(strips)):
        first = panel * PANEL
        live = strips[panel:]
        columns = [
            [
                jnp.broadcast_to(strip[:, first + k : first + k + 1], (PANEL, edge))
                for strip in live
            ]
            for k in range(PANEL)
        ]
        inside = (lanes >= first) & (lanes < first + PANEL)
        unit = (lanes == first + sublanes).astype(jnp.float32)
        live = [
            jnp.where(inside, unit if at == 0 else 0.0, strip) for at, strip in enumerate(live)
        ]
        pivots = jnp.ones((PANEL, edge), jnp.float32)
        for i in range(PANEL):
            pivot = jnp.broadcast_to(columns[i][0][i : i + 1, :], (PANEL, edge))
            pivots = jnp.where(sublanes == i, pivot, pivots)
            factor = 1.0 / pivot
            row = jnp.broadcast_to(live[0][i : i + 1, :], (PANEL, edge))
            heads = [
                jnp.broadcast_to(columns[k][0][i : i + 1, :], (PANEL, edge))
                for k in range(i + 1, PANEL)
            ]
            for at in range(len(live)):
                times = columns[i][at] * factor
                if at == 0:
                    times = jnp.where(sublanes > i, times, 0.0)
                live[at] = live[at] - times * row
                for k in range(i + 1, PANEL):
                    columns[k][at] = columns[k][at] - times * heads[k - i - 1]
        done.append(jnp.where(lanes <= first + sublanes, live[0] * lax.rsqrt(pivots), 0.0))
        strips = strips[: panel + 1] + live[1:]
    return jnp.concatenate(done, axis=0)


def basis_kernel(col_ref, blocks_ref, own_ref, other_ref, out_ref, held_ref):
    width = out_ref.shape[1]
    edge = blocks_ref.shape[2]
    half = width // edge
    size = 2 * width
    for block_row, block_col, holder, index in block_places(half):
        held_ref[
            block_row * edge : (block_row + 1) * edge, block_col * edge : (block_col + 1) * edge
        ] = blocks_ref[holder, index * edge : (index + 1) * edge, :]
    for start in range(0, size, edge):
        stop = start + edge
        inverse = invert_block(held_ref[start:stop, start:stop])
        if start:
            before = jnp.dot(
                inverse, held_ref[start:stop, :start],
                precision=HIGHEST, preferred_element_type=jnp.float32,
            )
            held_ref[start:stop, :start] = before
        held_ref[start:stop, start:stop] = inverse
        if stop < size:
            panel = lax.dot_general(
                held_ref[stop:, start:stop], inverse, (((1,), (1,)), ((), ())),
                precision=HIGHEST, preferred_element_type=jnp.float32,
            )
            held_ref[stop:, stop:] -= lax.dot_general(
                panel, panel, (((1,), (1,)), ((), ())),
                precision=HIGHEST, preferred_element_type=jnp.float32,
            )
            if start:
                held_ref[stop:, :start] -= jnp.dot(
                    panel, before, precision=HIGHEST, preferred_element_type=jnp.float32
                )
            held_ref[stop:, start:stop] = -jnp.dot(
                panel, inverse, precision=HIGHEST, preferred_element_type=jnp.float32
            )
            held_ref[start:stop, stop:] = jnp.zeros((edge, size - stop), jnp.float32)

    def add_half(rows_ref, first):
        own = held_ref[pl.ds(pl.multiple_of(col_ref[0] * width, width), width), first : first + width]
        high = own.astype(jnp.bfloat16)
        rest = own - high.astype(jnp.float32)
        middle = rest.astype(jnp.bfloat16)
        low = (rest - middle.astype(jnp.float32)).astype(jnp.bfloat16)
        total = jnp.zeros(out_ref.shape, jnp.float32)
        for piece in (low, middle, high):
            total += lax.dot_general(
                rows_ref[...], piece, (((1,), (1,)), ((), ())),
                preferred_element_type=jnp.float32,
            )
        return total

    @pl.when(col_ref[0] == 0)
    def _():
        out_ref[...] = add_half(own_ref, 0)

    @pl.when(col_ref[0] != 0)
    def _():
        out_ref[...] = add_half(other_ref, 0) + add_half(own_ref, width)


def block_places(half):
    places = []
    for holder in range(2):
        index = 0
        for block_col in range(half):
            for block_row in range(block_col, half):
                places.append((holder * half + block_row, holder * half + block_col, holder, index))
                index += 1
        for block_col in range(half // 2):
            for block_row in range(half):
                places.append(
                    (half + block_row, holder * (half // 2) + block_col, holder, index)
                )
                index += 1
    return places


def gram_kernel(
    owners, total_rows, chunk, own_ref, other_ref, blocks_ref, part_ref, sibling_ref, inbox_ref,
    pair_sems, half_sems, near_sems, far_sems, part_sems, sum_sems, pass_sems,
):
    me = lax.axis_index("blk")
    col = lax.axis_index("col")
    chips = owners // 2
    chip = me // 2
    core = lax.rem(me, 2)
    partner = {"blk": me, "col": 1 - col}
    sibling = {"blk": 2 * chip + 1 - core, "col": col}
    width = own_ref.shape[1]
    edge = blocks_ref.shape[2]
    half = width // edge
    span = sibling_ref.shape[0]
    reducers = span // chunk
    base = core * span

    def peer(q):
        return {"blk": 2 * q + core, "col": col}

    def remote(src, dst, sems, device):
        return pltpu.make_async_remote_copy(
            src_ref=src, dst_ref=dst, send_sem=sems[0], recv_sem=sems[1],
            device_id=device, device_id_type=pl.DeviceIdType.MESH,
        )

    def rows_at(start, count):
        return pl.ds(pl.multiple_of(start, 8), count)

    def rows_of(q):
        return rows_at(base + q * chunk, chunk)

    def part_copy(src, q):
        return remote(
            part_ref.at[rows_of(q)], inbox_ref.at[src],
            (part_sems.at[0, q], part_sems.at[1, src]), peer(q),
        )

    def sum_copy(src, q):
        rows = blocks_ref.at[col, rows_of(src)]
        return remote(rows, rows, (sum_sems.at[0, q], sum_sems.at[1, src]), peer(q))

    def pass_copy(holder, q):
        rows = blocks_ref.at[holder, rows_of(q)]
        return remote(rows, rows, (pass_sems.at[0, q], pass_sems.at[1, q]), partner)

    def share_copy(holder, side, sems):
        rows = blocks_ref.at[holder, rows_at(side * span, span)]
        return remote(rows, rows, (sems.at[0], sems.at[1]), sibling)

    def each(step, first=1):
        def turn(d, carry):
            step(d)
            return carry

        lax.fori_loop(first, chips, turn, 0)

    def ahead(d):
        return lax.rem(chip + d, chips)

    def behind(d):
        return lax.rem(chip + chips - d, chips)

    def each_reducer(step):
        def turn(d):
            q = ahead(d)

            @pl.when(q < reducers)
            def _():
                step(q)

        each(turn)

    barrier = pltpu.get_barrier_semaphore()

    def greet(device):
        pl.semaphore_signal(
            barrier, inc=1, device_id=device, device_id_type=pl.DeviceIdType.MESH
        )

    greet(partner)
    greet(sibling)
    each(lambda d: greet(peer(ahead(d))))
    pl.semaphore_wait(barrier, chips + 1)

    pair = remote(own_ref, other_ref, (pair_sems.at[0], pair_sems.at[1]), partner)
    pair.start()
    own = own_ref[...]
    own_gram = lax.dot_general(
        own, own, (((0,), (0,)), ((), ())), preferred_element_type=jnp.float32
    )
    index = 0
    for block_col in range(half):
        for block_row in range(block_col, half):
            part_ref[index * edge : (index + 1) * edge, :] = own_gram[
                block_row * edge : (block_row + 1) * edge, block_col * edge : (block_col + 1) * edge
            ]
            index += 1

    halves = remote(
        part_ref.at[rows_at((1 - core) * span, span)], sibling_ref,
        (half_sems.at[0], half_sems.at[1]), sibling,
    )

    pair.wait()
    other = other_ref[...]
    low_half = jnp.where(col == 0, own, other)
    high_half = jnp.where(col == 0, other, own)
    side = width // 2
    low_part = jnp.where(col == 0, low_half[:, :side], low_half[:, side:])
    cross = lax.dot_general(
        high_half, low_part, (((0,), (0,)), ((), ())), preferred_element_type=jnp.float32
    )
    for block_col in range(half // 2):
        for block_row in range(half):
            part_ref[index * edge : (index + 1) * edge, :] = cross[
                block_row * edge : (block_row + 1) * edge, block_col * edge : (block_col + 1) * edge
            ]
            index += 1
    halves.start()
    halves.wait()
    mine = rows_at(base, span)
    part_ref[mine] += sibling_ref[...]
    each_reducer(lambda q: part_copy(chip, q).start())

    @pl.when(chip < reducers)
    def _():
        def add(d, total):
            src = behind(d)
            part_copy(src, chip).wait_recv()
            return total + inbox_ref[src]

        total = lax.fori_loop(1, chips, add, part_ref[rows_of(chip)])
        blocks_ref[col, rows_of(chip)] = total / total_rows
        each(lambda d: sum_copy(chip, ahead(d)).start())
        pass_copy(col, chip).start()

    def hand_on(d):
        src = behind(d)

        @pl.when(src < reducers)
        def _():
            sum_copy(src, src).wait_recv()
            pass_copy(col, src).start()

    each(hand_on)
    near = share_copy(col, core, near_sems)
    near.start()

    def arrive(q, carry):
        pass_copy(1 - col, q).wait_recv()
        return carry

    lax.fori_loop(0, reducers, arrive, 0)
    far = share_copy(1 - col, core, far_sems)
    far.start()
    near.wait()
    far.wait()

    def leave(q, carry):
        pass_copy(col, q).wait_send()
        return carry

    lax.fori_loop(0, reducers, leave, 0)
    each_reducer(lambda q: part_copy(chip, q).wait_send())

    @pl.when(chip < reducers)
    def _():
        each(lambda d: sum_copy(chip, ahead(d)).wait_send())


def local(tiles, tile_rows, tile_cols, tile_count, sketch, variant_scale):
    width = sketch.shape[1]
    edge = tiles.shape[1]
    owners = lax.axis_size("blk")
    own_blocks = sketch.shape[0] // edge
    own_rows = RB_DEV
    slots = tiles.shape[0]
    every_slot = jnp.arange(slots, dtype=jnp.int32)
    owner_ids = jnp.arange(owners, dtype=jnp.int32)
    live = every_slot < tile_count[0]
    slot_owner = tile_cols // own_blocks
    slot_hits = (slot_owner[None, :] == owner_ids[:, None]) & live[None, :]
    wanted = jnp.max(jnp.where(slot_hits, (tile_cols % own_blocks)[None, :], 0), axis=1)
    places = jnp.arange(owners * own_rows, dtype=jnp.int32)
    place_hits = ((slot_owner * own_rows + tile_rows)[None, :] == places[:, None]) & live[None, :]
    slot_of = jnp.min(jnp.where(place_hits, every_slot[None, :], slots), axis=1)
    panel = (owners, edge, width)
    power_rows = pl.pallas_call(
        functools.partial(exchange_kernel, owners),
        out_shape=jax.ShapeDtypeStruct((own_rows * edge, width), jnp.bfloat16),
        in_specs=[SMEM_SPEC] + [VMEM_SPEC] * 4,
        out_specs=VMEM_SPEC,
        scratch_shapes=[
            pltpu.VMEM((owners, 1, edge), jnp.int32),
            pltpu.SMEM((owners, 1, edge), jnp.int32),
            pltpu.VMEM((slots + 1, edge, edge), jnp.bfloat16),
            pltpu.VMEM(panel, jnp.bfloat16),
            pltpu.VMEM(panel, jnp.bfloat16),
            pltpu.VMEM(panel, jnp.bfloat16),
            pltpu.VMEM(panel, jnp.float32),
            pltpu.VMEM((owners, edge, edge), jnp.float32),
            pltpu.VMEM((own_rows * edge, width), jnp.float32),
            pltpu.VMEM((own_rows * edge, width), jnp.bfloat16),
        ]
        + [pltpu.SemaphoreType.DMA((2, owners))] * 4
        + [pltpu.SemaphoreType.DMA],
        compiler_params=pltpu.CompilerParams(
            vmem_limit_bytes=VMEM_BYTES, collective_id=1, has_side_effects=True
        ),
        name="exchange_rows",
    )(
        slot_of,
        jnp.broadcast_to(wanted[:, None, None], (owners, 1, edge)),
        variant_scale.astype(jnp.float32).reshape(own_blocks, 1, edge),
        tiles,
        sketch.reshape(own_blocks, edge, width),
    )

    total_rows = own_rows * edge * owners
    half = width // edge
    depth = edge * (half * (half + 1) // 2 + half * half // 2)
    chips = owners // 2
    chunk = -(-depth // (16 * chips)) * 8
    span = -(-depth // (2 * chunk)) * chunk
    other_rows, blocks = pl.pallas_call(
        functools.partial(gram_kernel, owners, total_rows, chunk),
        out_shape=(
            jax.ShapeDtypeStruct(power_rows.shape, jnp.bfloat16),
            jax.ShapeDtypeStruct((2, 2 * span, edge), jnp.float32),
        ),
        in_specs=[VMEM_SPEC],
        out_specs=(VMEM_SPEC, VMEM_SPEC),
        scratch_shapes=[
            pltpu.VMEM((2 * span, edge), jnp.float32),
            pltpu.VMEM((span, edge), jnp.float32),
            pltpu.VMEM((chips, chunk, edge), jnp.float32),
        ]
        + [pltpu.SemaphoreType.DMA((2,))] * 4
        + [pltpu.SemaphoreType.DMA((2, chips))] * 3,
        compiler_params=pltpu.CompilerParams(
            vmem_limit_bytes=VMEM_BYTES, collective_id=0, has_side_effects=True
        ),
        name="gram_blocks",
    )(power_rows)
    return pl.pallas_call(
        basis_kernel,
        out_shape=jax.ShapeDtypeStruct((own_rows * edge, width), jnp.float32),
        in_specs=[SMEM_SPEC] + [VMEM_SPEC] * 3,
        out_specs=VMEM_SPEC,
        scratch_shapes=[pltpu.VMEM((2 * width, 2 * width), jnp.float32)],
        compiler_params=PARAMS,
        name="basis_rows",
    )(lax.axis_index("col").reshape(1).astype(jnp.int32), blocks, power_rows, other_rows)


def solution(mesh):
    placed = (P("blk", None, None), P("blk"), P("blk"), P("blk"), P("blk", "col"), P("blk"))
    return jax.shard_map(
        local, mesh=mesh, in_specs=placed, out_specs=P("blk", "col"), check_vma=False
    )
```

```python
import functools
import jax
import jax.numpy as jnp
from jax import lax
from jax.experimental import pallas as pl
from jax.experimental.pallas import tpu as pltpu
from jax.sharding import PartitionSpec as P

TPR = 6
RB_DEV = 4
PANEL = 8
VMEM_BYTES = 60 * 2**20
HIGHEST = lax.Precision.HIGHEST

SMEM_SPEC = pl.BlockSpec(memory_space=pltpu.SMEM)
VMEM_SPEC = pl.BlockSpec(memory_space=pltpu.VMEM)
PARAMS = pltpu.CompilerParams(vmem_limit_bytes=VMEM_BYTES)


def exchange_kernel(
    owners, slot_ref, wanted_ref, scale_ref, tiles_ref, sketch_ref, rows_ref,
    asked_in, asked, tile_set, send, fetched, arrived, sums, squares, acc, held,
    ask_sems, sketch_sems, term_sems, weight_sems, local_sem,
):
    me = lax.axis_index("blk")
    col = lax.axis_index("col")
    slots, edge, _ = tiles_ref.shape
    width = sketch_ref.shape[2]
    own_rows = acc.shape[0] // edge

    barrier = pltpu.get_barrier_semaphore()

    def each(step, first=1):
        def turn(d, carry):
            step(d)
            return carry

        lax.fori_loop(first, owners, turn, 0)

    span = owners // 2
    side = lax.div(me, span)
    place = lax.rem(me, span)

    def turn_of(d):
        near = lax.div(d - 1, span)
        return lax.rem(side + 1 - near, 2) * span, d - 1 - near * (span - 1)

    def ahead(d):
        first, step = turn_of(d)
        return first + lax.rem(place + step, span)

    def behind(d):
        first, step = turn_of(d)
        return first + lax.rem(place + span - step, span)

    def greet(d):
        pl.semaphore_signal(
            barrier, inc=1, device_id={"blk": ahead(d), "col": col},
            device_id_type=pl.DeviceIdType.MESH,
        )

    each(greet)

    def copy_of(source, target, sems):
        def make(src, q):
            return pltpu.make_async_remote_copy(
                src_ref=source.at[q], dst_ref=target.at[src],
                send_sem=sems.at[0, q], recv_sem=sems.at[1, src],
                device_id={"blk": q, "col": col}, device_id_type=pl.DeviceIdType.MESH,
            )

        return make

    ask_copy = copy_of(wanted_ref, asked_in, ask_sems)
    sketch_copy = copy_of(send, fetched, sketch_sems)
    term_copy = copy_of(send, arrived, term_sems)
    weight_copy = copy_of(send, fetched, weight_sems)

    tile_set[:slots] = tiles_ref[...]
    tile_set[slots] = jnp.zeros((edge, edge), jnp.bfloat16)
    asked_in[me] = wanted_ref[me]
    pl.semaphore_wait(barrier, owners - 1)
    each(lambda d: ask_copy(me, ahead(d)).start())
    each(lambda d: ask_copy(behind(d), me).wait_recv())
    into_scalars = pltpu.make_async_copy(asked_in, asked, local_sem)
    into_scalars.start()
    into_scalars.wait()

    lanes = lax.broadcasted_iota(jnp.int32, (edge, edge), 1)
    sublanes = lax.broadcasted_iota(jnp.int32, (edge, edge), 0)
    ones = jnp.ones((edge, edge), jnp.bfloat16)

    def served(q):
        block = asked[q, 0, 0]
        spread = jnp.broadcast_to(scale_ref[block], (edge, edge))
        diagonal = jnp.where(lanes == sublanes, spread, 0.0).astype(jnp.bfloat16)
        column = jnp.dot(diagonal, ones, preferred_element_type=jnp.float32)
        squares[q] = column * column
        rows = sketch_ref[block].astype(jnp.float32)
        return (rows * jnp.concatenate([column] * (width // edge), axis=1)).astype(jnp.bfloat16)

    def serve(d):
        q = ahead(d)
        send[q] = served(q)
        sketch_copy(me, q).start()

    each(serve)
    fetched[me] = served(me)

    def stack_of(owner):
        return jnp.concatenate(
            [tile_set[slot_ref[owner * own_rows + row]] for row in range(own_rows)], axis=0
        )

    def forward(copies):
        acc[...] = jnp.dot(stack_of(me), fetched[me], preferred_element_type=jnp.float32)

        def take(d):
            owner = behind(d)
            copies(owner, me).wait_recv()
            acc[...] += jnp.dot(
                stack_of(owner), fetched[owner], preferred_element_type=jnp.float32
            )

        each(take)

    forward(sketch_copy)
    held[...] = acc[...].astype(jnp.bfloat16)
    each(lambda d: sketch_copy(me, ahead(d)).wait_send())

    def term_of(owner):
        return lax.dot_general(
            stack_of(owner), held[...], (((0,), (0,)), ((), ())),
            preferred_element_type=jnp.float32,
        ).astype(jnp.bfloat16)

    def give(d):
        q = ahead(d)
        send[q] = term_of(q)
        term_copy(me, q).start()

    each(give)
    arrived[me] = term_of(me)

    def share(src, q):
        same = (asked[src, 0, 0] == asked[q, 0, 0]).astype(jnp.float32)
        return same * arrived[src].astype(jnp.float32)

    def begin(q, carry):
        sums[q] = share(me, q)
        return carry

    lax.fori_loop(0, owners, begin, 0)

    def gather(d):
        src = behind(d)
        term_copy(src, me).wait_recv()

        def add(q, carry):
            sums[q] += share(src, q)
            return carry

        lax.fori_loop(0, owners, add, 0)

    each(gather)
    each(lambda d: term_copy(me, ahead(d)).wait_send())

    def weighted(q):
        square = jnp.concatenate([squares[q]] * (width // edge), axis=1)
        return (square * sums[q]).astype(jnp.bfloat16)

    def give_weighted(d):
        q = ahead(d)
        send[q] = weighted(q)
        weight_copy(me, q).start()

    each(give_weighted)
    fetched[me] = weighted(me)
    forward(weight_copy)
    rows_ref[...] = acc[...].astype(jnp.bfloat16)
    each(lambda d: ask_copy(me, ahead(d)).wait_send())
    each(lambda d: weight_copy(me, ahead(d)).wait_send())


def invert_block(block):
    edge = block.shape[0]
    lanes = lax.broadcasted_iota(jnp.int32, (PANEL, edge), 1)
    sublanes = lax.broadcasted_iota(jnp.int32, (PANEL, edge), 0)
    strips = [block[start : start + PANEL, :] for start in range(0, edge, PANEL)]
    done = []
    for panel in range(len(strips)):
        first = panel * PANEL
        live = strips[panel:]
        columns = [
            [
                jnp.broadcast_to(strip[:, first + k : first + k + 1], (PANEL, edge))
                for strip in live
            ]
            for k in range(PANEL)
        ]
        inside = (lanes >= first) & (lanes < first + PANEL)
        unit = (lanes == first + sublanes).astype(jnp.float32)
        live = [
            jnp.where(inside, unit if at == 0 else 0.0, strip) for at, strip in enumerate(live)
        ]
        pivots = jnp.ones((PANEL, edge), jnp.float32)
        for i in range(PANEL):
            pivot = jnp.broadcast_to(columns[i][0][i : i + 1, :], (PANEL, edge))
            pivots = jnp.where(sublanes == i, pivot, pivots)
            factor = 1.0 / pivot
            row = jnp.broadcast_to(live[0][i : i + 1, :], (PANEL, edge))
            heads = [
                jnp.broadcast_to(columns[k][0][i : i + 1, :], (PANEL, edge))
                for k in range(i + 1, PANEL)
            ]
            for at in range(len(live)):
                times = columns[i][at] * factor
                if at == 0:
                    times = jnp.where(sublanes > i, times, 0.0)
                live[at] = live[at] - times * row
                for k in range(i + 1, PANEL):
                    columns[k][at] = columns[k][at] - times * heads[k - i - 1]
        done.append(jnp.where(lanes <= first + sublanes, live[0] * lax.rsqrt(pivots), 0.0))
        strips = strips[: panel + 1] + live[1:]
    return jnp.concatenate(done, axis=0)


def basis_kernel(col_ref, blocks_ref, own_ref, other_ref, out_ref, held_ref):
    width = out_ref.shape[1]
    edge = blocks_ref.shape[2]
    half = width // edge
    size = 2 * width
    for block_row, block_col, holder, index in block_places(half):
        held_ref[
            block_row * edge : (block_row + 1) * edge, block_col * edge : (block_col + 1) * edge
        ] = blocks_ref[holder, index * edge : (index + 1) * edge, :]
    for start in range(0, size, edge):
        stop = start + edge
        inverse = invert_block(held_ref[start:stop, start:stop])
        if start:
            before = jnp.dot(
                inverse, held_ref[start:stop, :start],
                precision=HIGHEST, preferred_element_type=jnp.float32,
            )
            held_ref[start:stop, :start] = before
        held_ref[start:stop, start:stop] = inverse
        if stop < size:
            panel = lax.dot_general(
                held_ref[stop:, start:stop], inverse, (((1,), (1,)), ((), ())),
                precision=HIGHEST, preferred_element_type=jnp.float32,
            )
            held_ref[stop:, stop:] -= lax.dot_general(
                panel, panel, (((1,), (1,)), ((), ())),
                precision=HIGHEST, preferred_element_type=jnp.float32,
            )
            if start:
                held_ref[stop:, :start] -= jnp.dot(
                    panel, before, precision=HIGHEST, preferred_element_type=jnp.float32
                )
            held_ref[stop:, start:stop] = -jnp.dot(
                panel, inverse, precision=HIGHEST, preferred_element_type=jnp.float32
            )
            held_ref[start:stop, stop:] = jnp.zeros((edge, size - stop), jnp.float32)

    def add_half(rows_ref, first):
        own = held_ref[pl.ds(pl.multiple_of(col_ref[0] * width, width), width), first : first + width]
        high = own.astype(jnp.bfloat16)
        rest = own - high.astype(jnp.float32)
        middle = rest.astype(jnp.bfloat16)
        low = (rest - middle.astype(jnp.float32)).astype(jnp.bfloat16)
        total = jnp.zeros(out_ref.shape, jnp.float32)
        for piece in (low, middle, high):
            total += lax.dot_general(
                rows_ref[...], piece, (((1,), (1,)), ((), ())),
                preferred_element_type=jnp.float32,
            )
        return total

    @pl.when(col_ref[0] == 0)
    def _():
        out_ref[...] = add_half(own_ref, 0)

    @pl.when(col_ref[0] != 0)
    def _():
        out_ref[...] = add_half(other_ref, 0) + add_half(own_ref, width)


def block_places(half):
    places = []
    for holder in range(2):
        index = 0
        for block_col in range(half):
            for block_row in range(block_col, half):
                places.append((holder * half + block_row, holder * half + block_col, holder, index))
                index += 1
        for block_col in range(half // 2):
            for block_row in range(half):
                places.append(
                    (half + block_row, holder * (half // 2) + block_col, holder, index)
                )
                index += 1
    return places


def gram_kernel(
    owners, total_rows, chunk, own_ref, other_ref, blocks_ref, part_ref, sibling_ref, inbox_ref,
    pair_sems, half_sems, near_sems, far_sems, part_sems, sum_sems, pass_sems,
):
    me = lax.axis_index("blk")
    col = lax.axis_index("col")
    chips = owners // 2
    chip = me // 2
    core = lax.rem(me, 2)
    partner = {"blk": me, "col": 1 - col}
    sibling = {"blk": 2 * chip + 1 - core, "col": col}
    width = own_ref.shape[1]
    edge = blocks_ref.shape[2]
    half = width // edge
    span = sibling_ref.shape[0]
    reducers = span // chunk
    base = core * span

    def peer(q):
        return {"blk": 2 * q + core, "col": col}

    def remote(src, dst, sems, device):
        return pltpu.make_async_remote_copy(
            src_ref=src, dst_ref=dst, send_sem=sems[0], recv_sem=sems[1],
            device_id=device, device_id_type=pl.DeviceIdType.MESH,
        )

    def rows_at(start, count):
        return pl.ds(pl.multiple_of(start, 8), count)

    def rows_of(q):
        return rows_at(base + q * chunk, chunk)

    def part_copy(src, q):
        return remote(
            part_ref.at[rows_of(q)], inbox_ref.at[src],
            (part_sems.at[0, q], part_sems.at[1, src]), peer(q),
        )

    def sum_copy(src, q):
        rows = blocks_ref.at[col, rows_of(src)]
        return remote(rows, rows, (sum_sems.at[0, q], sum_sems.at[1, src]), peer(q))

    def pass_copy(holder, q):
        rows = blocks_ref.at[holder, rows_of(q)]
        return remote(rows, rows, (pass_sems.at[0, q], pass_sems.at[1, q]), partner)

    def share_copy(holder, side, sems):
        rows = blocks_ref.at[holder, rows_at(side * span, span)]
        return remote(rows, rows, (sems.at[0], sems.at[1]), sibling)

    def each(step, first=1):
        def turn(d, carry):
            step(d)
            return carry

        lax.fori_loop(first, chips, turn, 0)

    def ahead(d):
        return lax.rem(chip + d, chips)

    def behind(d):
        return lax.rem(chip + chips - d, chips)

    def each_reducer(step):
        def turn(d):
            q = ahead(d)

            @pl.when(q < reducers)
            def _():
                step(q)

        each(turn)

    barrier = pltpu.get_barrier_semaphore()

    def greet(device):
        pl.semaphore_signal(
            barrier, inc=1, device_id=device, device_id_type=pl.DeviceIdType.MESH
        )

    greet(partner)
    greet(sibling)
    each(lambda d: greet(peer(ahead(d))))
    pl.semaphore_wait(barrier, chips + 1)

    pair = remote(own_ref, other_ref, (pair_sems.at[0], pair_sems.at[1]), partner)
    pair.start()
    own = own_ref[...]
    own_gram = lax.dot_general(
        own, own, (((0,), (0,)), ((), ())), preferred_element_type=jnp.float32
    )
    index = 0
    for block_col in range(half):
        for block_row in range(block_col, half):
            part_ref[index * edge : (index + 1) * edge, :] = own_gram[
                block_row * edge : (block_row + 1) * edge, block_col * edge : (block_col + 1) * edge
            ]
            index += 1

    halves = remote(
        part_ref.at[rows_at((1 - core) * span, span)], sibling_ref,
        (half_sems.at[0], half_sems.at[1]), sibling,
    )

    pair.wait()
    other = other_ref[...]
    low_half = jnp.where(col == 0, own, other)
    high_half = jnp.where(col == 0, other, own)
    side = width // 2
    low_part = jnp.where(col == 0, low_half[:, :side], low_half[:, side:])
    cross = lax.dot_general(
        high_half, low_part, (((0,), (0,)), ((), ())), preferred_element_type=jnp.float32
    )
    for block_col in range(half // 2):
        for block_row in range(half):
            part_ref[index * edge : (index + 1) * edge, :] = cross[
                block_row * edge : (block_row + 1) * edge, block_col * edge : (block_col + 1) * edge
            ]
            index += 1
    halves.start()
    halves.wait()
    mine = rows_at(base, span)
    part_ref[mine] += sibling_ref[...]
    each_reducer(lambda q: part_copy(chip, q).start())

    @pl.when(chip < reducers)
    def _():
        def add(d, total):
            src = behind(d)
            part_copy(src, chip).wait_recv()
            return total + inbox_ref[src]

        total = lax.fori_loop(1, chips, add, part_ref[rows_of(chip)])
        blocks_ref[col, rows_of(chip)] = total / total_rows
        each(lambda d: sum_copy(chip, ahead(d)).start())
        pass_copy(col, chip).start()

    def hand_on(d):
        src = behind(d)

        @pl.when(src < reducers)
        def _():
            sum_copy(src, src).wait_recv()
            pass_copy(col, src).start()

    each(hand_on)
    near = share_copy(col, core, near_sems)
    near.start()

    def arrive(q, carry):
        pass_copy(1 - col, q).wait_recv()
        return carry

    lax.fori_loop(0, reducers, arrive, 0)
    far = share_copy(1 - col, core, far_sems)
    far.start()
    near.wait()
    far.wait()

    def leave(q, carry):
        pass_copy(col, q).wait_send()
        return carry

    lax.fori_loop(0, reducers, leave, 0)
    each_reducer(lambda q: part_copy(chip, q).wait_send())

    @pl.when(chip < reducers)
    def _():
        each(lambda d: sum_copy(chip, ahead(d)).wait_send())


def local(tiles, tile_rows, tile_cols, tile_count, sketch, variant_scale):
    width = sketch.shape[1]
    edge = tiles.shape[1]
    owners = lax.axis_size("blk")
    own_blocks = sketch.shape[0] // edge
    own_rows = RB_DEV
    slots = tiles.shape[0]
    every_slot = jnp.arange(slots, dtype=jnp.int32)
    owner_ids = jnp.arange(owners, dtype=jnp.int32)
    live = every_slot < tile_count[0]
    slot_owner = tile_cols // own_blocks
    slot_hits = (slot_owner[None, :] == owner_ids[:, None]) & live[None, :]
    wanted = jnp.max(jnp.where(slot_hits, (tile_cols % own_blocks)[None, :], 0), axis=1)
    places = jnp.arange(owners * own_rows, dtype=jnp.int32)
    place_hits = ((slot_owner * own_rows + tile_rows)[None, :] == places[:, None]) & live[None, :]
    slot_of = jnp.min(jnp.where(place_hits, every_slot[None, :], slots), axis=1)
    panel = (owners, edge, width)
    power_rows = pl.pallas_call(
        functools.partial(exchange_kernel, owners),
        out_shape=jax.ShapeDtypeStruct((own_rows * edge, width), jnp.bfloat16),
        in_specs=[SMEM_SPEC] + [VMEM_SPEC] * 4,
        out_specs=VMEM_SPEC,
        scratch_shapes=[
            pltpu.VMEM((owners, 1, edge), jnp.int32),
            pltpu.SMEM((owners, 1, edge), jnp.int32),
            pltpu.VMEM((slots + 1, edge, edge), jnp.bfloat16),
            pltpu.VMEM(panel, jnp.bfloat16),
            pltpu.VMEM(panel, jnp.bfloat16),
            pltpu.VMEM(panel, jnp.bfloat16),
            pltpu.VMEM(panel, jnp.float32),
            pltpu.VMEM((owners, edge, edge), jnp.float32),
            pltpu.VMEM((own_rows * edge, width), jnp.float32),
            pltpu.VMEM((own_rows * edge, width), jnp.bfloat16),
        ]
        + [pltpu.SemaphoreType.DMA((2, owners))] * 4
        + [pltpu.SemaphoreType.DMA],
        compiler_params=pltpu.CompilerParams(
            vmem_limit_bytes=VMEM_BYTES, collective_id=1, has_side_effects=True
        ),
        name="exchange_rows",
    )(
        slot_of,
        jnp.broadcast_to(wanted[:, None, None], (owners, 1, edge)),
        variant_scale.astype(jnp.float32).reshape(own_blocks, 1, edge),
        tiles,
        sketch.reshape(own_blocks, edge, width),
    )

    total_rows = own_rows * edge * owners
    half = width // edge
    depth = edge * (half * (half + 1) // 2 + half * half // 2)
    chips = owners // 2
    chunk = -(-depth // (16 * chips)) * 8
    span = -(-depth // (2 * chunk)) * chunk
    other_rows, blocks = pl.pallas_call(
        functools.partial(gram_kernel, owners, total_rows, chunk),
        out_shape=(
            jax.ShapeDtypeStruct(power_rows.shape, jnp.bfloat16),
            jax.ShapeDtypeStruct((2, 2 * span, edge), jnp.float32),
        ),
        in_specs=[VMEM_SPEC],
        out_specs=(VMEM_SPEC, VMEM_SPEC),
        scratch_shapes=[
            pltpu.VMEM((2 * span, edge), jnp.float32),
            pltpu.VMEM((span, edge), jnp.float32),
            pltpu.VMEM((chips, chunk, edge), jnp.float32),
        ]
        + [pltpu.SemaphoreType.DMA((2,))] * 4
        + [pltpu.SemaphoreType.DMA((2, chips))] * 3,
        compiler_params=pltpu.CompilerParams(
            vmem_limit_bytes=VMEM_BYTES, collective_id=0, has_side_effects=True
        ),
        name="gram_blocks",
    )(power_rows)
    return pl.pallas_call(
        basis_kernel,
        out_shape=jax.ShapeDtypeStruct((own_rows * edge, width), jnp.float32),
        in_specs=[SMEM_SPEC] + [VMEM_SPEC] * 3,
        out_specs=VMEM_SPEC,
        scratch_shapes=[pltpu.VMEM((2 * width, 2 * width), jnp.float32)],
        compiler_params=PARAMS,
        name="basis_rows",
    )(lax.axis_index("col").reshape(1).astype(jnp.int32), blocks, power_rows, other_rows)


def solution(mesh):
    placed = (P("blk", None, None), P("blk"), P("blk"), P("blk"), P("blk", "col"), P("blk"))
    return jax.shard_map(
        local, mesh=mesh, in_specs=placed, out_specs=P("blk", "col"), check_vma=False
    )
```

```python
import functools
import jax
import jax.numpy as jnp
from jax import lax
from jax.experimental import pallas as pl
from jax.experimental.pallas import tpu as pltpu
from jax.sharding import PartitionSpec as P

TPR = 6
RB_DEV = 4
PANEL = 8
VMEM_BYTES = 60 * 2**20
HIGHEST = lax.Precision.HIGHEST

SMEM_SPEC = pl.BlockSpec(memory_space=pltpu.SMEM)
VMEM_SPEC = pl.BlockSpec(memory_space=pltpu.VMEM)
PARAMS = pltpu.CompilerParams(vmem_limit_bytes=VMEM_BYTES)


def exchange_kernel(
    owners, slot_ref, wanted_ref, scale_ref, tiles_ref, sketch_ref, rows_ref,
    asked_in, asked, tile_set, send, fetched, arrived, sums, squares, acc, held,
    ask_sems, sketch_sems, term_sems, weight_sems, local_sem,
):
    me = lax.axis_index("blk")
    col = lax.axis_index("col")
    slots, edge, _ = tiles_ref.shape
    width = sketch_ref.shape[2]
    own_rows = acc.shape[0] // edge

    barrier = pltpu.get_barrier_semaphore()

    def each(step, first=1):
        def turn(d, carry):
            step(d)
            return carry

        lax.fori_loop(first, owners, turn, 0)

    span = owners // 2
    side = lax.div(me, span)
    place = lax.rem(me, span)

    def turn_of(d):
        near = lax.div(d - 1, span)
        return lax.rem(side + 1 - near, 2) * span, d - 1 - near * (span - 1)

    def ahead(d):
        first, step = turn_of(d)
        return first + lax.rem(place + step, span)

    def behind(d):
        first, step = turn_of(d)
        return first + lax.rem(place + span - step, span)

    def greet(d):
        pl.semaphore_signal(
            barrier, inc=1, device_id={"blk": ahead(d), "col": col},
            device_id_type=pl.DeviceIdType.MESH,
        )

    each(greet)

    def copy_of(source, target, sems):
        def make(src, q):
            return pltpu.make_async_remote_copy(
                src_ref=source.at[q], dst_ref=target.at[src],
                send_sem=sems.at[0, q], recv_sem=sems.at[1, src],
                device_id={"blk": q, "col": col}, device_id_type=pl.DeviceIdType.MESH,
            )

        return make

    ask_copy = copy_of(wanted_ref, asked_in, ask_sems)
    sketch_copy = copy_of(send, fetched, sketch_sems)
    term_copy = copy_of(send, arrived, term_sems)
    weight_copy = copy_of(send, fetched, weight_sems)

    tile_set[:slots] = tiles_ref[...]
    tile_set[slots] = jnp.zeros((edge, edge), jnp.bfloat16)
    asked_in[me] = wanted_ref[me]
    pl.semaphore_wait(barrier, owners - 1)
    each(lambda d: ask_copy(me, ahead(d)).start())
    each(lambda d: ask_copy(behind(d), me).wait_recv())
    into_scalars = pltpu.make_async_copy(asked_in, asked, local_sem)
    into_scalars.start()
    into_scalars.wait()

    lanes = lax.broadcasted_iota(jnp.int32, (edge, edge), 1)
    sublanes = lax.broadcasted_iota(jnp.int32, (edge, edge), 0)
    ones = jnp.ones((edge, edge), jnp.bfloat16)

    def served(q):
        block = asked[q, 0, 0]
        spread = jnp.broadcast_to(scale_ref[block], (edge, edge))
        diagonal = jnp.where(lanes == sublanes, spread, 0.0).astype(jnp.bfloat16)
        column = jnp.dot(diagonal, ones, preferred_element_type=jnp.float32)
        squares[q] = column * column
        rows = sketch_ref[block].astype(jnp.float32)
        return (rows * jnp.concatenate([column] * (width // edge), axis=1)).astype(jnp.bfloat16)

    def serve(d):
        q = ahead(d)
        send[q] = served(q)
        sketch_copy(me, q).start()

    each(serve)
    fetched[me] = served(me)

    def stack_of(owner):
        return jnp.concatenate(
            [tile_set[slot_ref[owner * own_rows + row]] for row in range(own_rows)], axis=0
        )

    def forward(copies):
        acc[...] = jnp.dot(stack_of(me), fetched[me], preferred_element_type=jnp.float32)

        def take(d):
            owner = behind(d)
            copies(owner, me).wait_recv()
            acc[...] += jnp.dot(
                stack_of(owner), fetched[owner], preferred_element_type=jnp.float32
            )

        each(take)

    forward(sketch_copy)
    held[...] = acc[...].astype(jnp.bfloat16)
    each(lambda d: sketch_copy(me, ahead(d)).wait_send())

    def term_of(owner):
        return lax.dot_general(
            stack_of(owner), held[...], (((0,), (0,)), ((), ())),
            preferred_element_type=jnp.float32,
        ).astype(jnp.bfloat16)

    def give(d):
        q = ahead(d)
        send[q] = term_of(q)
        term_copy(me, q).start()

    each(give)
    arrived[me] = term_of(me)

    def share(src, q):
        same = (asked[src, 0, 0] == asked[q, 0, 0]).astype(jnp.float32)
        return same * arrived[src].astype(jnp.float32)

    def begin(q, carry):
        sums[q] = share(me, q)
        return carry

    lax.fori_loop(0, owners, begin, 0)

    def gather(d):
        src = behind(d)
        term_copy(src, me).wait_recv()

        def add(q, carry):
            sums[q] += share(src, q)
            return carry

        lax.fori_loop(0, owners, add, 0)

    each(gather)
    each(lambda d: term_copy(me, ahead(d)).wait_send())

    def weighted(q):
        square = jnp.concatenate([squares[q]] * (width // edge), axis=1)
        return (square * sums[q]).astype(jnp.bfloat16)

    def give_weighted(d):
        q = ahead(d)
        send[q] = weighted(q)
        weight_copy(me, q).start()

    each(give_weighted)
    fetched[me] = weighted(me)
    forward(weight_copy)
    rows_ref[...] = acc[...].astype(jnp.bfloat16)
    each(lambda d: ask_copy(me, ahead(d)).wait_send())
    each(lambda d: weight_copy(me, ahead(d)).wait_send())


def invert_block(block):
    edge = block.shape[0]
    lanes = lax.broadcasted_iota(jnp.int32, (PANEL, edge), 1)
    sublanes = lax.broadcasted_iota(jnp.int32, (PANEL, edge), 0)
    strips = [block[start : start + PANEL, :] for start in range(0, edge, PANEL)]
    done = []
    for panel in range(len(strips)):
        first = panel * PANEL
        live = strips[panel:]
        columns = [
            [
                jnp.broadcast_to(strip[:, first + k : first + k + 1], (PANEL, edge))
                for strip in live
            ]
            for k in range(PANEL)
        ]
        inside = (lanes >= first) & (lanes < first + PANEL)
        unit = (lanes == first + sublanes).astype(jnp.float32)
        live = [
            jnp.where(inside, unit if at == 0 else 0.0, strip) for at, strip in enumerate(live)
        ]
        pivots = jnp.ones((PANEL, edge), jnp.float32)
        for i in range(PANEL):
            pivot = jnp.broadcast_to(columns[i][0][i : i + 1, :], (PANEL, edge))
            pivots = jnp.where(sublanes == i, pivot, pivots)
            factor = pl.reciprocal(pivot)
            row = jnp.broadcast_to(live[0][i : i + 1, :], (PANEL, edge))
            heads = [
                jnp.broadcast_to(columns[k][0][i : i + 1, :], (PANEL, edge))
                for k in range(i + 1, PANEL)
            ]
            for at in range(len(live)):
                times = columns[i][at] * factor
                if at == 0:
                    times = jnp.where(sublanes > i, times, 0.0)
                live[at] = live[at] - times * row
                for k in range(i + 1, PANEL):
                    columns[k][at] = columns[k][at] - times * heads[k - i - 1]
        done.append(jnp.where(lanes <= first + sublanes, live[0] * lax.rsqrt(pivots), 0.0))
        strips = strips[: panel + 1] + live[1:]
    return jnp.concatenate(done, axis=0)


def basis_kernel(col_ref, blocks_ref, own_ref, other_ref, out_ref, held_ref):
    width = out_ref.shape[1]
    edge = blocks_ref.shape[2]
    half = width // edge
    size = 2 * width
    for block_row, block_col, holder, index in block_places(half):
        held_ref[
            block_row * edge : (block_row + 1) * edge, block_col * edge : (block_col + 1) * edge
        ] = blocks_ref[holder, index * edge : (index + 1) * edge, :]
    for start in range(0, size, edge):
        stop = start + edge
        inverse = invert_block(held_ref[start:stop, start:stop])
        if start:
            before = jnp.dot(
                inverse, held_ref[start:stop, :start],
                precision=HIGHEST, preferred_element_type=jnp.float32,
            )
            held_ref[start:stop, :start] = before
        held_ref[start:stop, start:stop] = inverse
        if stop < size:
            panel = lax.dot_general(
                held_ref[stop:, start:stop], inverse, (((1,), (1,)), ((), ())),
                precision=HIGHEST, preferred_element_type=jnp.float32,
            )
            held_ref[stop:, stop:] -= lax.dot_general(
                panel, panel, (((1,), (1,)), ((), ())),
                precision=HIGHEST, preferred_element_type=jnp.float32,
            )
            if start:
                held_ref[stop:, :start] -= jnp.dot(
                    panel, before, precision=HIGHEST, preferred_element_type=jnp.float32
                )
            held_ref[stop:, start:stop] = -jnp.dot(
                panel, inverse, precision=HIGHEST, preferred_element_type=jnp.float32
            )
            held_ref[start:stop, stop:] = jnp.zeros((edge, size - stop), jnp.float32)

    def add_half(rows_ref, first):
        own = held_ref[pl.ds(pl.multiple_of(col_ref[0] * width, width), width), first : first + width]
        high = own.astype(jnp.bfloat16)
        rest = own - high.astype(jnp.float32)
        middle = rest.astype(jnp.bfloat16)
        low = (rest - middle.astype(jnp.float32)).astype(jnp.bfloat16)
        total = jnp.zeros(out_ref.shape, jnp.float32)
        for piece in (low, middle, high):
            total += lax.dot_general(
                rows_ref[...], piece, (((1,), (1,)), ((), ())),
                preferred_element_type=jnp.float32,
            )
        return total

    @pl.when(col_ref[0] == 0)
    def _():
        out_ref[...] = add_half(own_ref, 0)

    @pl.when(col_ref[0] != 0)
    def _():
        out_ref[...] = add_half(other_ref, 0) + add_half(own_ref, width)


def block_places(half):
    places = []
    for holder in range(2):
        index = 0
        for block_col in range(half):
            for block_row in range(block_col, half):
                places.append((holder * half + block_row, holder * half + block_col, holder, index))
                index += 1
        for block_col in range(half // 2):
            for block_row in range(half):
                places.append(
                    (half + block_row, holder * (half // 2) + block_col, holder, index)
                )
                index += 1
    return places


def gram_kernel(
    owners, total_rows, chunk, own_ref, other_ref, blocks_ref, part_ref, sibling_ref, inbox_ref,
    pair_sems, half_sems, near_sems, far_sems, part_sems, sum_sems, pass_sems,
):
    me = lax.axis_index("blk")
    col = lax.axis_index("col")
    chips = owners // 2
    chip = me // 2
    core = lax.rem(me, 2)
    partner = {"blk": me, "col": 1 - col}
    sibling = {"blk": 2 * chip + 1 - core, "col": col}
    width = own_ref.shape[1]
    edge = blocks_ref.shape[2]
    half = width // edge
    span = sibling_ref.shape[0]
    reducers = span // chunk
    base = core * span

    def peer(q):
        return {"blk": 2 * q + core, "col": col}

    def remote(src, dst, sems, device):
        return pltpu.make_async_remote_copy(
            src_ref=src, dst_ref=dst, send_sem=sems[0], recv_sem=sems[1],
            device_id=device, device_id_type=pl.DeviceIdType.MESH,
        )

    def rows_at(start, count):
        return pl.ds(pl.multiple_of(start, 8), count)

    def rows_of(q):
        return rows_at(base + q * chunk, chunk)

    def part_copy(src, q):
        return remote(
            part_ref.at[rows_of(q)], inbox_ref.at[src],
            (part_sems.at[0, q], part_sems.at[1, src]), peer(q),
        )

    def sum_copy(src, q):
        rows = blocks_ref.at[col, rows_of(src)]
        return remote(rows, rows, (sum_sems.at[0, q], sum_sems.at[1, src]), peer(q))

    def pass_copy(holder, q):
        rows = blocks_ref.at[holder, rows_of(q)]
        return remote(rows, rows, (pass_sems.at[0, q], pass_sems.at[1, q]), partner)

    def share_copy(holder, side, sems):
        rows = blocks_ref.at[holder, rows_at(side * span, span)]
        return remote(rows, rows, (sems.at[0], sems.at[1]), sibling)

    def each(step, first=1):
        def turn(d, carry):
            step(d)
            return carry

        lax.fori_loop(first, chips, turn, 0)

    def ahead(d):
        return lax.rem(chip + d, chips)

    def behind(d):
        return lax.rem(chip + chips - d, chips)

    def each_reducer(step):
        def turn(d):
            q = ahead(d)

            @pl.when(q < reducers)
            def _():
                step(q)

        each(turn)

    barrier = pltpu.get_barrier_semaphore()

    def greet(device):
        pl.semaphore_signal(
            barrier, inc=1, device_id=device, device_id_type=pl.DeviceIdType.MESH
        )

    greet(partner)
    greet(sibling)
    each(lambda d: greet(peer(ahead(d))))
    pl.semaphore_wait(barrier, chips + 1)

    pair = remote(own_ref, other_ref, (pair_sems.at[0], pair_sems.at[1]), partner)
    pair.start()
    own = own_ref[...]
    own_gram = lax.dot_general(
        own, own, (((0,), (0,)), ((), ())), preferred_element_type=jnp.float32
    )
    index = 0
    for block_col in range(half):
        for block_row in range(block_col, half):
            part_ref[index * edge : (index + 1) * edge, :] = own_gram[
                block_row * edge : (block_row + 1) * edge, block_col * edge : (block_col + 1) * edge
            ]
            index += 1

    halves = remote(
        part_ref.at[rows_at((1 - core) * span, span)], sibling_ref,
        (half_sems.at[0], half_sems.at[1]), sibling,
    )

    pair.wait()
    other = other_ref[...]
    low_half = jnp.where(col == 0, own, other)
    high_half = jnp.where(col == 0, other, own)
    side = width // 2
    low_part = jnp.where(col == 0, low_half[:, :side], low_half[:, side:])
    cross = lax.dot_general(
        high_half, low_part, (((0,), (0,)), ((), ())), preferred_element_type=jnp.float32
    )
    for block_col in range(half // 2):
        for block_row in range(half):
            part_ref[index * edge : (index + 1) * edge, :] = cross[
                block_row * edge : (block_row + 1) * edge, block_col * edge : (block_col + 1) * edge
            ]
            index += 1
    halves.start()
    halves.wait()
    mine = rows_at(base, span)
    part_ref[mine] += sibling_ref[...]
    each_reducer(lambda q: part_copy(chip, q).start())

    @pl.when(chip < reducers)
    def _():
        def add(d, total):
            src = behind(d)
            part_copy(src, chip).wait_recv()
            return total + inbox_ref[src]

        total = lax.fori_loop(1, chips, add, part_ref[rows_of(chip)])
        blocks_ref[col, rows_of(chip)] = total / total_rows
        each(lambda d: sum_copy(chip, ahead(d)).start())
        pass_copy(col, chip).start()

    def hand_on(d):
        src = behind(d)

        @pl.when(src < reducers)
        def _():
            sum_copy(src, src).wait_recv()
            pass_copy(col, src).start()

    each(hand_on)
    near = share_copy(col, core, near_sems)
    near.start()

    def arrive(q, carry):
        pass_copy(1 - col, q).wait_recv()
        return carry

    lax.fori_loop(0, reducers, arrive, 0)
    far = share_copy(1 - col, core, far_sems)
    far.start()
    near.wait()
    far.wait()

    def leave(q, carry):
        pass_copy(col, q).wait_send()
        return carry

    lax.fori_loop(0, reducers, leave, 0)
    each_reducer(lambda q: part_copy(chip, q).wait_send())

    @pl.when(chip < reducers)
    def _():
        each(lambda d: sum_copy(chip, ahead(d)).wait_send())


def local(tiles, tile_rows, tile_cols, tile_count, sketch, variant_scale):
    width = sketch.shape[1]
    edge = tiles.shape[1]
    owners = lax.axis_size("blk")
    own_blocks = sketch.shape[0] // edge
    own_rows = RB_DEV
    slots = tiles.shape[0]
    every_slot = jnp.arange(slots, dtype=jnp.int32)
    owner_ids = jnp.arange(owners, dtype=jnp.int32)
    live = every_slot < tile_count[0]
    slot_owner = tile_cols // own_blocks
    slot_hits = (slot_owner[None, :] == owner_ids[:, None]) & live[None, :]
    wanted = jnp.max(jnp.where(slot_hits, (tile_cols % own_blocks)[None, :], 0), axis=1)
    places = jnp.arange(owners * own_rows, dtype=jnp.int32)
    place_hits = ((slot_owner * own_rows + tile_rows)[None, :] == places[:, None]) & live[None, :]
    slot_of = jnp.min(jnp.where(place_hits, every_slot[None, :], slots), axis=1)
    panel = (owners, edge, width)
    power_rows = pl.pallas_call(
        functools.partial(exchange_kernel, owners),
        out_shape=jax.ShapeDtypeStruct((own_rows * edge, width), jnp.bfloat16),
        in_specs=[SMEM_SPEC] + [VMEM_SPEC] * 4,
        out_specs=VMEM_SPEC,
        scratch_shapes=[
            pltpu.VMEM((owners, 1, edge), jnp.int32),
            pltpu.SMEM((owners, 1, edge), jnp.int32),
            pltpu.VMEM((slots + 1, edge, edge), jnp.bfloat16),
            pltpu.VMEM(panel, jnp.bfloat16),
            pltpu.VMEM(panel, jnp.bfloat16),
            pltpu.VMEM(panel, jnp.bfloat16),
            pltpu.VMEM(panel, jnp.float32),
            pltpu.VMEM((owners, edge, edge), jnp.float32),
            pltpu.VMEM((own_rows * edge, width), jnp.float32),
            pltpu.VMEM((own_rows * edge, width), jnp.bfloat16),
        ]
        + [pltpu.SemaphoreType.DMA((2, owners))] * 4
        + [pltpu.SemaphoreType.DMA],
        compiler_params=pltpu.CompilerParams(
            vmem_limit_bytes=VMEM_BYTES, collective_id=1, has_side_effects=True
        ),
        name="exchange_rows",
    )(
        slot_of,
        jnp.broadcast_to(wanted[:, None, None], (owners, 1, edge)),
        variant_scale.astype(jnp.float32).reshape(own_blocks, 1, edge),
        tiles,
        sketch.reshape(own_blocks, edge, width),
    )

    total_rows = own_rows * edge * owners
    half = width // edge
    depth = edge * (half * (half + 1) // 2 + half * half // 2)
    chips = owners // 2
    chunk = -(-depth // (16 * chips)) * 8
    span = -(-depth // (2 * chunk)) * chunk
    other_rows, blocks = pl.pallas_call(
        functools.partial(gram_kernel, owners, total_rows, chunk),
        out_shape=(
            jax.ShapeDtypeStruct(power_rows.shape, jnp.bfloat16),
            jax.ShapeDtypeStruct((2, 2 * span, edge), jnp.float32),
        ),
        in_specs=[VMEM_SPEC],
        out_specs=(VMEM_SPEC, VMEM_SPEC),
        scratch_shapes=[
            pltpu.VMEM((2 * span, edge), jnp.float32),
            pltpu.VMEM((span, edge), jnp.float32),
            pltpu.VMEM((chips, chunk, edge), jnp.float32),
        ]
        + [pltpu.SemaphoreType.DMA((2,))] * 4
        + [pltpu.SemaphoreType.DMA((2, chips))] * 3,
        compiler_params=pltpu.CompilerParams(
            vmem_limit_bytes=VMEM_BYTES, collective_id=0, has_side_effects=True
        ),
        name="gram_blocks",
    )(power_rows)
    return pl.pallas_call(
        basis_kernel,
        out_shape=jax.ShapeDtypeStruct((own_rows * edge, width), jnp.float32),
        in_specs=[SMEM_SPEC] + [VMEM_SPEC] * 3,
        out_specs=VMEM_SPEC,
        scratch_shapes=[pltpu.VMEM((2 * width, 2 * width), jnp.float32)],
        compiler_params=PARAMS,
        name="basis_rows",
    )(lax.axis_index("col").reshape(1).astype(jnp.int32), blocks, power_rows, other_rows)


def solution(mesh):
    placed = (P("blk", None, None), P("blk"), P("blk"), P("blk"), P("blk", "col"), P("blk"))
    return jax.shard_map(
        local, mesh=mesh, in_specs=placed, out_specs=P("blk", "col"), check_vma=False
    )
```
